32 devices in a mesh: groups: 2 (over y), sub: 4 (over z), scen: 2 (over x), half: 2 (over core).
Axes of the slice: x: 2, y: 2, z: 4, core: 2. Of those that a mesh axis runs over, the one named last changes fastest.
Arguments:
- inverses: bfloat16 [16, 512, 512], P(('groups', 'sub', 'half')), parts along dimension 0
- cotangent: bfloat16 [16, 64, 512], P(('groups', 'sub', 'half'), 'scen'), parts along dimension 0, may hold values from -6 to 6
- subnet_sizes: int32 [16], P(('groups', 'sub', 'half')), parts along dimension 0, may hold values from 256 to 512, as said below
- slot_into: int32 [16, 8, 8], P(('groups', 'sub', 'half')), parts along dimension 0, may hold values from 0 to 511, as said below
- slot_from: int32 [16, 8, 8], P(('groups', 'sub', 'half')), parts along dimension 0, may hold values from -1 to 511, as said below
- offsets: int32 [16, 8, 8], P(('groups', 'sub', 'half')), parts along dimension 0, may hold values from 2 to 4
- weights: float32 [16, 8, 8], P(('groups', 'sub', 'half')), parts along dimension 0, may hold values from 0 to 1
- admittance: float32 [16, 8, 8], P(('groups', 'sub', 'half')), parts along dimension 0, may hold values from 0.5 to 2
- fault_bus: int32 [128], P(('groups', 'scen')), parts along dimension 0, may hold values from 0 to 4095, as said below
Outputs:
- first_adjoint: bfloat16 [16, 64, 512], P(('groups', 'sub', 'half'), 'scen'), parts along dimension 0
- fault_grad: float32 [8, 128], P(None, ('groups', 'scen')), parts along dimension 1
The draws below stay inside these ranges and needn't reach their ends.
There are 2 independent parts, one for each index of `groups`. The reference program is written for one: setup_inputs(seed, part) draws one part's arguments, and reference() takes and returns one part's arrays. A program takes and returns all parts, laid end to end along the dimension named above; each array names one. Nothing has to cross between parts.
Inputs may be any that keep to these rules, and one draw needn't show every extreme that they name: `subnet_sizes`: some subnetwork has exactly 512 live nodes. `slot_into`: names a live node of the sending device; 0 in slots that are empty. `slot_from`: names a live node of the receiving device; for each pair of devices the used slots come first; in every draw some receiving device has all 8 slots used from every sender. `fault_bus`: names a live node.
All inputs are finite; a program needn't handle non-finite values.
Results may differ from the reference program's by a relative error of at most 0.009.
Values may be sent and summed in bfloat16 or wider, within the bound.
No kernel may reach another device: no remote copies, remote signals or barrier semaphores. Data moves between devices by JAX's collectives and lax.ppermute only.
A program may use at most 64 MiB of HBM per device.

```python
import math
import jax
import jax.numpy as jnp
from jax import lax

NB = 512
SUB_DEV = 1
CAP = 8
STEPS = 8
OWNERS = 8
SUBS = 8
SCEN = 64


def sizes_of(key):
    first, second = jax.random.split(jax.random.fold_in(key, 11))
    counts = jax.random.randint(first, (SUBS,), NB // 2, NB + 1)
    chosen = jax.random.randint(second, (), 0, SUBS)
    return counts.at[chosen].set(NB).astype(jnp.int32)


def slots_of(key):
    node_sizes = sizes_of(key)
    keys = jax.random.split(jax.random.fold_in(key, 22), 6)
    counts = jax.random.randint(keys[0], (OWNERS, OWNERS), 0, CAP + 1)
    hot_owner = jax.random.randint(keys[1], (), 0, OWNERS)
    counts = counts.at[:, hot_owner].set(CAP)
    is_used = jnp.arange(CAP)[None, None, :] < counts[:, :, None]
    owner_ids = jnp.arange(OWNERS)
    into_block = jax.random.randint(keys[2], (OWNERS, OWNERS, CAP), 0, SUB_DEV)
    into_raw = jax.random.randint(keys[3], (OWNERS, OWNERS, CAP), 0, 2 ** 20)
    into_sub = owner_ids[:, None, None] * SUB_DEV + into_block
    into_local = into_block * NB + into_raw % node_sizes[into_sub]
    from_block = jax.random.randint(keys[4], (OWNERS, OWNERS, CAP), 0, SUB_DEV)
    from_raw = jax.random.randint(keys[5], (OWNERS, OWNERS, CAP), 0, 2 ** 20)
    from_sub = owner_ids[None, :, None] * SUB_DEV + from_block
    from_local = from_block * NB + from_raw % node_sizes[from_sub]
    into_local = jnp.where(is_used, into_local, 0)
    from_local = jnp.where(is_used, from_local, -1)
    return (into_local.astype(jnp.int32), jnp.transpose(from_local, (1, 0, 2)).astype(jnp.int32))


def draw_subnet_sizes(key, part):
    return sizes_of(key)


def draw_slot_into(key, part):
    return slots_of(key)[0]


def draw_slot_from(key, part):
    return slots_of(key)[1]


def draw_fault_bus(key, part):
    node_sizes = sizes_of(key)
    key = jax.random.fold_in(key, 33)
    first, second = jax.random.split(key)
    which = jax.random.randint(first, (SCEN,), 0, SUBS)
    raw = jax.random.randint(second, (SCEN,), 0, 2 ** 20)
    return (which * NB + raw % node_sizes[which]).astype(jnp.int32)


def draw_inverses(key, part):
    key = jax.random.fold_in(key, 44)
    keys = jax.random.split(key, 2)
    diagonal = jnp.exp(jax.random.uniform(keys[0], (SUBS, NB), minval=0.0, maxval=math.log(2.0)))
    spread = jax.random.normal(keys[1], (SUBS, NB, NB))
    matrix = spread * (1.0 / math.sqrt(NB)) + jnp.eye(NB, dtype=jnp.float32)[None, :, :] * diagonal[:, :, None]
    return matrix.astype(jnp.bfloat16)


def set_ends(entries, stream_key, least, high):
    longest = entries.shape.index(max(entries.shape))
    spots = []
    for shift in (0, 1):
        where = [jax.random.randint(jax.random.fold_in(stream_key, axis), (), 0, length) for axis, length in enumerate(entries.shape)]
        where[longest] = (where[longest] + shift) % entries.shape[longest]
        spots.append(tuple(where))
    return entries.at[spots[0]].set(least).at[spots[1]].set(high)


def block_scale(stream_key, extent, cuts, least, high):
    loudness, own = 1.0, jax.random.fold_in(stream_key, 6)
    for axis_at, parts in cuts:
        steps = jnp.exp(jax.random.uniform(jax.random.fold_in(own, axis_at), (parts,), jnp.float32, least / len(cuts), high / len(cuts)))
        loudness = loudness * jnp.repeat(steps, extent[axis_at] // parts).reshape([-1 if axis == axis_at else 1 for axis in range(len(extent))])
    return loudness


def scatter_about(rng, extent, scale, limit, cuts=(), kind=jnp.bfloat16):
    values = scale * jax.random.normal(rng, extent, jnp.float32)
    if cuts:
        values = values * block_scale(rng, extent, cuts, -0.22, 0.18)
    return jnp.clip(values, -limit, limit).astype(kind)


def setup_inputs(seed: int = 0, part: int = 0) -> dict:
    splits = jax.random.split(jax.random.key(seed), 10)
    own_keys = jax.random.split(jax.random.fold_in(splits[9], part), 10)
    return {
        "inverses": draw_inverses(jax.random.fold_in(jax.random.fold_in(splits[9], part), 71), part),
        "cotangent": scatter_about(own_keys[1], (SUBS, SCEN, NB), 1.0, 6.0, ((0, 8), (1, 2))),
        "subnet_sizes": draw_subnet_sizes(jax.random.fold_in(jax.random.fold_in(splits[9], part), 71), part),
        "slot_into": draw_slot_into(jax.random.fold_in(jax.random.fold_in(splits[9], part), 71), part),
        "slot_from": draw_slot_from(jax.random.fold_in(jax.random.fold_in(splits[9], part), 71), part),
        "offsets": set_ends(jax.random.randint(own_keys[5], (OWNERS, OWNERS, CAP), 2, 5), jax.random.fold_in(own_keys[5], 1), 2, 4).astype(jnp.int32),
        "weights": jnp.clip(1.0 * jax.random.uniform(own_keys[6], (OWNERS, OWNERS, CAP), jnp.float32) ** block_scale(own_keys[6], (OWNERS, OWNERS, CAP), ((0, 8),), -0.2, 0.2), 0.0, 1.0),
        "admittance": jnp.clip(jnp.exp(math.log(2.0) - 1.3862944 * jax.random.uniform(own_keys[7], (OWNERS, OWNERS, CAP), jnp.float32) ** block_scale(own_keys[7], (OWNERS, OWNERS, CAP), ((0, 8),), -0.2, 0.2)), 0.5, 2.0),
        "fault_bus": draw_fault_bus(jax.random.fold_in(jax.random.fold_in(splits[9], part), 71), part),
    }


def reference(inverses, cotangent, subnet_sizes, slot_into, slot_from, offsets, weights, admittance, fault_bus):
    span = SUB_DEV * NB
    owner_ids = jnp.arange(OWNERS, dtype=jnp.int32)
    into_global = (owner_ids[:, None, None] * span + slot_into).reshape(-1)
    from_turned = jnp.transpose(slot_from, (1, 0, 2))
    is_used = (from_turned >= 0).reshape(-1)
    from_global = (owner_ids[None, :, None] * span + jnp.maximum(from_turned, 0)).reshape(-1)
    delay_steps = jnp.transpose(offsets, (1, 0, 2)).reshape(-1)
    fraction = jnp.transpose(weights, (1, 0, 2)).reshape(-1)
    conduct = jnp.transpose(admittance, (1, 0, 2)).reshape(-1) * is_used.astype(jnp.float32)
    into_sub = into_global // NB
    into_node = into_global % NB
    from_sub = from_global // NB
    from_node = from_global % NB
    active = (jnp.arange(NB, dtype=jnp.int32)[None, :] < subnet_sizes[:, None]).astype(jnp.float32)
    inverse_wide = inverses.astype(jnp.float32)
    fault_sub = fault_bus // NB
    fault_node = fault_bus % NB
    columns = jnp.arange(SCEN, dtype=jnp.int32)
    sent_values = {}
    fault_rows = {}
    first_adjoint = None
    for step_now in range(STEPS - 1, -1, -1):
        history = jnp.zeros((SUBS, SCEN, NB), jnp.float32)
        terms = jnp.zeros((into_global.shape[0], SCEN), jnp.float32)
        for source_step in range(step_now + 2, min(step_now + 6, STEPS)):
            step_gap = source_step - step_now
            factor = conduct * (fraction * (delay_steps == step_gap).astype(jnp.float32)
                                + (1.0 - fraction) * (delay_steps + 1 == step_gap).astype(jnp.float32))
            terms = terms + factor[:, None] * sent_values[source_step].astype(jnp.float32)
        history = history.at[from_sub, :, from_node].add(terms)
        if step_now == STEPS - 1:
            history = history + cotangent.astype(jnp.float32)
        driving = (history * active[:, None, :]).astype(jnp.bfloat16)
        adjoint = jnp.einsum("jsn,jnm->jsm", driving.astype(jnp.float32), inverse_wide,
                             precision=lax.Precision.HIGHEST)
        adjoint = (adjoint * active[:, None, :]).astype(jnp.bfloat16)
        sent_values[step_now] = adjoint[into_sub, :, into_node]
        fault_rows[step_now] = adjoint[fault_sub, columns, fault_node].astype(jnp.float32)
        first_adjoint = adjoint
    fault_grad = jnp.stack([fault_rows[index] for index in range(STEPS)])
    return first_adjoint, fault_grad
```

```python
import jax
import jax.numpy as jnp
import numpy as np
from jax import lax
from jax.experimental import pallas as pl
from jax.experimental.pallas import tpu as pltpu
from jax.sharding import PartitionSpec as P

STEPS = 8
LANES = 128
OWNER_AXES = ("sub", "half")
VARIANTS = (
    (2, 3, 0, 2),
    (2, 2, 3, 3),
    (4, 5, 0, 4),
    (2, 2, 0, 2),
    (0, 3, 0, 0),
    (4, 5, 3, 4),
)
NT = (((1,), (1,)), ((), ()))
TN = (((0,), (0,)), ((), ()))


def dot(left, right, dims=(((1,), (0,)), ((), ()))):
    return lax.dot_general(left, right, dims, preferred_element_type=jnp.float32)


def spread_matrix(column_count, slot_count):
    spread = np.zeros((LANES, (len(VARIANTS) + 1) * LANES), np.float32)
    for variant, gaps in enumerate(VARIANTS):
        for quarter, gap in enumerate(gaps):
            if gap:
                lane = variant * LANES + quarter * column_count
                for piece in range(3):
                    row = slot_count + column_count + 3 * (gap - 2) + piece
                    spread[row, lane : lane + column_count] = 1
    for lane in range(LANES):
        spread[slot_count + lane % column_count, len(VARIANTS) * LANES + lane] = 1
    return spread


def column_of(ref, peers, depth):
    eye = lax.broadcasted_iota(jnp.int32, (depth, depth), 0) == lax.broadcasted_iota(
        jnp.int32, (depth, depth), 1
    )
    rows = [
        jnp.where(eye, jnp.broadcast_to(ref[0, peer : peer + 1, :].astype(jnp.float32), (depth, depth)), 0.0)
        for peer in range(peers)
    ]
    return jnp.sum(jnp.concatenate(rows, axis=0), axis=1, keepdims=True)


def pick_kernel(
    size_ref, owner_ref, inverse_hbm, cotangent_ref, into_ref, from_ref, offset_ref, weight_ref, admit_ref, bus_ref,
    message_ref, rows_ref, inverse_ref, semaphore,
):
    load = pltpu.make_async_copy(inverse_hbm.at[0], inverse_ref, semaphore)
    load.start()
    _, peers, depth = into_ref.shape
    slots = peers * depth
    columns, nodes = cotangent_ref.shape[1:]
    live = size_ref[0]
    lane = lax.broadcasted_iota(jnp.int32, (slots, nodes), 1)
    lane_f = lane.astype(jnp.float32)
    alive = lane < live
    into = column_of(into_ref, peers, depth)
    source = column_of(from_ref, peers, depth)
    delay = column_of(offset_ref, peers, depth)
    weight = column_of(weight_ref, peers, depth)
    admit = column_of(admit_ref, peers, depth)
    recv_hot = jnp.where((source == lane_f) & alive, 1.0, 0.0).astype(jnp.bfloat16)
    send_hot = jnp.where(into == lane_f, 1.0, 0.0).astype(jnp.bfloat16)
    driving = jnp.where(alive[:columns], cotangent_ref[0].astype(jnp.float32), 0.0).astype(jnp.bfloat16)
    bus = (bus_ref[...] - owner_ref[0] * nodes).astype(jnp.float32)
    eye = lax.broadcasted_iota(jnp.int32, (columns, columns), 0) == lax.broadcasted_iota(
        jnp.int32, (columns, columns), 1
    )
    bus = jnp.sum(jnp.where(eye, jnp.broadcast_to(bus, (columns, columns)), 0.0), axis=1, keepdims=True)
    fault_hot = jnp.where(bus == lane_f[:columns], 1.0, 0.0).astype(jnp.bfloat16)
    hot = jnp.concatenate([send_hot, fault_hot], axis=0)
    conduct = jnp.where(source >= 0, admit, 0.0)
    near, far = conduct * weight, conduct * (1.0 - weight)
    factors = [
        jnp.where(delay == 2, near, 0.0),
        jnp.where(delay == 3, near, 0.0) + jnp.where(delay == 2, far, 0.0),
        jnp.where(delay == 4, near, 0.0) + jnp.where(delay == 3, far, 0.0),
        jnp.where(delay == 4, far, 0.0),
    ]
    spot = lax.broadcasted_iota(jnp.int32, (slots, LANES), 1)
    params = jnp.zeros((slots, LANES), jnp.float32)
    for index, factor in enumerate(factors):
        rest = factor
        for piece in range(3):
            part = rest.astype(jnp.bfloat16).astype(jnp.float32)
            rest = rest - part
            params = jnp.where(spot == slots + columns + 3 * index + piece, part, params)
    load.wait()
    stack = jnp.concatenate([recv_hot, driving], axis=0)
    picked = dot(stack, inverse_ref[...])
    lane = lax.broadcasted_iota(jnp.int32, picked.shape, 1)
    picked = jnp.where(lane < live, picked, 0.0).astype(jnp.bfloat16)
    rows_ref[...] = picked[:slots]
    picked = jnp.concatenate([picked, jnp.zeros((LANES - slots - columns, nodes), jnp.bfloat16)], axis=0)
    body = dot(hot, picked, NT)
    body = body + jnp.concatenate([params, jnp.zeros((columns, LANES), jnp.float32)], axis=0)
    message_ref[...] = body.astype(jnp.bfloat16)


def march_kernel(place_ref, gathered_ref, spread_ref, rows_ref, first_ref, fault_ref, last_ref):
    owners, height, _ = gathered_ref.shape
    slots = rows_ref.shape[0]
    columns = height - slots
    depth = slots // owners
    place = place_ref[0]

    def exchange(parts):
        return [
            jnp.concatenate([part[depth * owner : depth * (owner + 1)] for part in parts], axis=0)
            for owner in range(owners)
        ]

    def rounded(value):
        return value.astype(jnp.bfloat16).astype(jnp.float32)

    blocks = [gathered_ref[lax.bitwise_xor(jnp.int32(owner), place)] for owner in range(owners)]
    count = len(VARIANTS)
    spread = [dot(block[:slots], spread_ref[...]) for block in blocks]
    factor = [[part[:, LANES * v : LANES * (v + 1)] for part in spread] for v in range(count)]
    seven = exchange([part[:, LANES * count :] for part in spread])
    system = [block[:, :slots] for block in blocks]

    drive = [
        jnp.concatenate([factor[0][o] * seven[o], factor[1][o] * seven[o]], axis=1).astype(jnp.bfloat16)
        for o in range(owners)
    ]
    result = [dot(system[o], drive[o]) for o in range(owners)]
    fault_a = sum(part[slots:, :LANES] for part in result[1:]) + result[0][slots:, :LANES]
    arrived = exchange([rounded(part) for part in result])
    low = [part[:, :LANES] for part in arrived]
    high = [part[:, LANES:] for part in arrived]
    drive = [
        (factor[2][o] * seven[o] + factor[3][o] * low[o] + factor[4][o] * high[o]).astype(jnp.bfloat16)
        for o in range(owners)
    ]
    later = [factor[5][o] * high[o] for o in range(owners)]
    result = [dot(system[o], drive[o]) for o in range(owners)]
    fault_b = sum(part[slots:] for part in result[1:]) + result[0][slots:]
    arrived = exchange([rounded(part) for part in result])
    later = [later[o] + factor[1][o] * arrived[o] for o in range(owners)]
    drive = [(part + pltpu.roll(part, 2 * columns, 1)).astype(jnp.bfloat16) for part in later]
    for o in range(owners):
        last_ref[o] = drive[o]
    own = last_ref[place]
    adjoint = dot(own, rows_ref[...], TN)
    first_ref[0] = adjoint[columns : 2 * columns].astype(jnp.bfloat16)
    fault_c = sum(dot(system[o][slots:], drive[o]) for o in range(owners))
    fault_s = sum(block[slots:].astype(jnp.float32) for block in blocks)

    lane = lax.broadcasted_iota(jnp.int32, (columns, LANES), 1)
    mine = lane % columns == lax.broadcasted_iota(jnp.int32, (columns, LANES), 0)

    def row(value):
        return rounded(jnp.sum(jnp.where(mine, value, 0.0), axis=0, keepdims=True))

    row_a, row_b, row_c, row_s = row(fault_a), row(fault_b), row(fault_c), row(fault_s)

    def back(value, quarters):
        return pltpu.roll(value, LANES - quarters * columns, 1)

    table = [
        back(row_c, 1),
        row_c,
        back(row_b, 1),
        row_b,
        back(row_a, 1),
        row_a,
        jnp.zeros_like(row_a),
        back(row_s, 2),
    ]
    step = lax.broadcasted_iota(jnp.int32, (STEPS, LANES), 0)
    total = jnp.zeros((STEPS, LANES), jnp.float32)
    for index, value in enumerate(table):
        total = jnp.where(step == index, jnp.broadcast_to(value, total.shape), total)
    fault_ref[...] = total[:, :columns]


def gathered_plan(
    inverses, cotangent, subnet_sizes, slot_into, slot_from, offsets, weights, admittance, fault_bus
):
    _, columns, nodes = cotangent.shape
    owners, depth = slot_into.shape[1:]
    slots = owners * depth
    height = slots + columns
    owner = lax.axis_index(OWNER_AXES).astype(jnp.int32)[None]
    vmem = pl.BlockSpec(memory_space=pltpu.VMEM)
    smem = pl.BlockSpec(memory_space=pltpu.SMEM)
    message, rows = pl.pallas_call(
        pick_kernel,
        out_shape=(
            jax.ShapeDtypeStruct((height, LANES), jnp.bfloat16),
            jax.ShapeDtypeStruct((slots, nodes), jnp.bfloat16),
        ),
        in_specs=[smem, smem, pl.BlockSpec(memory_space=pl.ANY)] + [vmem] * 7,
        out_specs=(vmem, vmem),
        scratch_shapes=[pltpu.VMEM((nodes, nodes), jnp.bfloat16), pltpu.SemaphoreType.DMA],
        name="pick",
    )(
        subnet_sizes, owner, inverses, cotangent, slot_into, slot_from, offsets, weights, admittance, fault_bus[None],
    )
    bits = owners.bit_length() - 1
    held = message[None]
    for bit in range(bits):
        other = lax.ppermute(held, OWNER_AXES, [(i, i ^ (1 << bit)) for i in range(owners)])
        held = jnp.concatenate([held, other], axis=0)
    spread = jnp.asarray(spread_matrix(columns, slots), jnp.bfloat16)
    return pl.pallas_call(
        march_kernel,
        out_shape=(
            jax.ShapeDtypeStruct((1, columns, nodes), jnp.bfloat16),
            jax.ShapeDtypeStruct((STEPS, columns), jnp.float32),
        ),
        in_specs=[smem, vmem, vmem, vmem],
        out_specs=(vmem, vmem),
        scratch_shapes=[pltpu.VMEM((owners, slots, LANES), jnp.bfloat16)],
        name="march",
    )(owner, held, spread, rows)


def exchanged_plan(
    inverses, cotangent, subnet_sizes, slot_into, slot_from, offsets, weights, admittance, fault_bus
):
    block_count, column_count, node_count = cotangent.shape
    owner_count = lax.axis_size(OWNER_AXES)
    slot_depth = slot_into.shape[2]
    slot_count = owner_count * slot_depth
    local_span = block_count * node_count
    active = (jnp.arange(node_count, dtype=jnp.int32)[None, :] < subnet_sizes[:, None]).astype(
        jnp.float32
    )
    node_ids = jnp.arange(local_span, dtype=jnp.int32)[None, :]
    send_hot = (slot_into.reshape(slot_count)[:, None] == node_ids).astype(jnp.bfloat16)
    send_hot = send_hot.reshape(slot_count, block_count, node_count)
    from_local = slot_from.reshape(slot_count)
    is_used = (from_local >= 0).astype(jnp.float32)
    recv_hot = (
        (from_local[:, None] == node_ids)
        .astype(jnp.float32)
        .reshape(slot_count, block_count, node_count)
    )
    delay_steps = offsets.reshape(slot_count)
    fraction = weights.reshape(slot_count)
    conduct = admittance.reshape(slot_count) * is_used
    arrivals = {}
    results = {}
    for step_now in range(STEPS - 1, -1, -1):
        history = jnp.zeros((block_count, column_count, node_count), jnp.float32)
        terms = jnp.zeros((column_count, slot_count), jnp.float32)
        present = False
        for source_step in range(step_now + 2, min(step_now + 6, STEPS)):
            step_gap = source_step - step_now
            factor = conduct * (
                fraction * (delay_steps == step_gap).astype(jnp.float32)
                + (1.0 - fraction) * (delay_steps + 1 == step_gap).astype(jnp.float32)
            )
            terms = terms + factor[None, :] * arrivals[source_step].astype(jnp.float32)
            present = True
        if present:
            history = jnp.einsum("sk,kjn->jsn", terms, recv_hot, precision=lax.Precision.HIGHEST)
        if step_now == STEPS - 1:
            history = cotangent.astype(jnp.float32)
        driving = (history * active[:, None, :]).astype(jnp.bfloat16)
        adjoint = jnp.einsum("jsn,jnm->jsm", driving, inverses, preferred_element_type=jnp.float32)
        results[step_now] = (adjoint * active[:, None, :]).astype(jnp.bfloat16)
        if step_now >= 2:
            picked = jnp.einsum(
                "jsn,kjn->sk", results[step_now], send_hot, preferred_element_type=jnp.float32
            )
            arrivals[step_now] = lax.all_to_all(
                picked.astype(jnp.bfloat16)[None], OWNER_AXES, split_axis=2, concat_axis=2, tiled=True
            )[0]
    owner_index = lax.axis_index(OWNER_AXES)
    local_bus = fault_bus - owner_index * local_span
    owned = (local_bus >= 0) & (local_bus < local_span)
    clamped = jnp.clip(local_bus, 0, local_span - 1)
    position = (
        clamped // node_count * column_count * node_count
        + jnp.arange(column_count, dtype=jnp.int32) * node_count
        + clamped % node_count
    )
    sensitivity = jnp.stack(
        [
            jnp.where(
                owned, jnp.take(results[index].reshape(-1), position).astype(jnp.float32), 0.0
            )
            for index in range(STEPS)
        ]
    )
    return results[0], lax.psum(sensitivity, OWNER_AXES)


def per_device(*arrays):
    blocks, columns, nodes = arrays[1].shape
    owners, depth = arrays[3].shape[1:]
    slots = owners * depth
    fits = (
        blocks == 1
        and columns * 4 == LANES
        and depth == 8
        and owners & (owners - 1) == 0
        and slots + columns + 12 <= LANES
        and nodes % LANES == 0
    )
    return gathered_plan(*arrays) if fits else exchanged_plan(*arrays)


def solution(mesh):
    return jax.shard_map(
        per_device,
        mesh=mesh,
        in_specs=(
            P(("groups", "sub", "half"), None, None),
            P(("groups", "sub", "half"), "scen", None),
            P(("groups", "sub", "half")),
            P(("groups", "sub", "half"), None, None),
            P(("groups", "sub", "half"), None, None),
            P(("groups", "sub", "half"), None, None),
            P(("groups", "sub", "half"), None, None),
            P(("groups", "sub", "half"), None, None),
            P(("groups", "scen")),
        ),
        out_specs=(P(("groups", "sub", "half"), "scen", None), P(None, ("groups", "scen"))),
        check_vma=False,
    )
```

```python
import jax
import jax.numpy as jnp
import numpy as np
from jax import lax
from jax.experimental import pallas as pl
from jax.experimental.pallas import tpu as pltpu
from jax.sharding import PartitionSpec as P

STEPS = 8
LANES = 128
VMEM_LIMIT = 16 * 2**20
BANDS = 2
OWNER_AXES = ("sub", "half")
VARIANTS = (
    (2, 3, 0, 2),
    (2, 2, 3, 3),
    (4, 5, 0, 4),
    (2, 2, 0, 2),
    (0, 3, 0, 0),
    (4, 5, 3, 4),
)
NT = (((1,), (1,)), ((), ()))


def dot(left, right, dims=(((1,), (0,)), ((), ()))):
    return lax.dot_general(left, right, dims, preferred_element_type=jnp.float32)


def spread_matrix(column_count, owners):
    half = LANES // 2
    spread = np.zeros((LANES, (len(VARIANTS) + 2) * LANES), np.float32)
    for variant, gaps in enumerate(VARIANTS):
        for quarter, gap in enumerate(gaps):
            lane = variant * LANES + quarter * column_count
            for piece in range(3 * (gap - 2), 3 * (gap - 1)) if gap else ():
                for owner in range(owners):
                    spread[piece // 8 * half + owner * 8 + piece % 8, lane : lane + column_count] = 1
    for lane in range(LANES):
        for part in range(2):
            start = half + part * column_count
            spread[start + lane % column_count, (len(VARIANTS) + part) * LANES + lane] = 1
    return spread


def exchange_masks(owners):
    masks = []
    reach = owners // 2
    while reach > 1:
        masks.append(reach + 1)
        reach //= 2
    return masks + [1]


def held_spots(owners):
    masks = exchange_masks(owners)
    place_of = {}
    for place in range(owners):
        apart = 0
        for bit, mask in enumerate(masks):
            if place >> bit & 1:
                apart ^= mask
        place_of[apart] = place
    return [place_of[1 << bit] for bit in range(len(masks))]


def column_of(ref, peers, depth):
    eye = lax.broadcasted_iota(jnp.int32, (depth, depth), 0) == lax.broadcasted_iota(
        jnp.int32, (depth, depth), 1
    )
    rows = [
        jnp.where(eye, jnp.broadcast_to(ref[0, peer : peer + 1, :].astype(jnp.float32), (depth, depth)), 0.0)
        for peer in range(peers)
    ]
    return jnp.sum(jnp.concatenate(rows, axis=0), axis=1, keepdims=True)


def owner_here():
    return lax.axis_index(OWNER_AXES[0]) * lax.axis_size(OWNER_AXES[1]) + lax.axis_index(OWNER_AXES[1])


def pick_kernel(
    size_ref, inverse_hbm, cotangent_hbm, into_hbm, from_hbm, offset_hbm, weight_hbm, admit_hbm, bus_hbm,
    message_ref, rows_ref,
    inverse_ref, cotangent_ref, into_ref, from_ref, offset_ref, weight_ref, admit_ref, bus_ref, semaphores,
):
    sources = (into_hbm, from_hbm, offset_hbm, weight_hbm, admit_hbm, bus_hbm, cotangent_hbm)
    targets = (into_ref, from_ref, offset_ref, weight_ref, admit_ref, bus_ref, cotangent_ref)
    loads = [
        pltpu.make_async_copy(source, target, semaphores.at[index])
        for index, (source, target) in enumerate(zip(sources, targets))
    ]
    for load in loads:
        load.start()
    nodes = inverse_ref.shape[0]
    bands = [pl.ds(nodes // BANDS * band, nodes // BANDS) for band in range(BANDS)]
    wide = [
        pltpu.make_async_copy(inverse_hbm.at[0, band], inverse_ref.at[band], semaphores.at[len(loads) + index])
        for index, band in enumerate(bands)
    ]
    for load in wide:
        load.start()
    _, peers, depth = into_ref.shape
    slots = peers * depth
    columns = cotangent_ref.shape[1]
    lane = lax.broadcasted_iota(jnp.int32, (slots, nodes), 1)
    lane_f = lane.astype(jnp.float32)
    for load in loads:
        load.wait()
    live = size_ref[...]
    alive = lane < live
    into = column_of(into_ref, peers, depth)
    source = column_of(from_ref, peers, depth)
    delay = column_of(offset_ref, peers, depth)
    weight = column_of(weight_ref, peers, depth)
    admit = column_of(admit_ref, peers, depth)
    recv_hot = jnp.where((source == lane_f) & alive, 1.0, 0.0).astype(jnp.bfloat16)
    send_hot = jnp.where(into == lane_f, 1.0, 0.0).astype(jnp.bfloat16)
    driving = jnp.where(alive[:columns], cotangent_ref[0].astype(jnp.float32), 0.0).astype(jnp.bfloat16)
    bus = (bus_ref[...] - owner_here() * nodes).astype(jnp.float32)
    eye = lax.broadcasted_iota(jnp.int32, (columns, columns), 0) == lax.broadcasted_iota(
        jnp.int32, (columns, columns), 1
    )
    bus = jnp.sum(jnp.where(eye, jnp.broadcast_to(bus, (columns, columns)), 0.0), axis=1, keepdims=True)
    fault_hot = jnp.where(bus == lane_f[:columns], 1.0, 0.0).astype(jnp.bfloat16)
    conduct = jnp.where(source >= 0, admit, 0.0)
    near, far = conduct * weight, conduct * (1.0 - weight)
    factors = [
        jnp.where(delay == 2, near, 0.0),
        jnp.where(delay == 3, near, 0.0) + jnp.where(delay == 2, far, 0.0),
        jnp.where(delay == 4, near, 0.0) + jnp.where(delay == 3, far, 0.0),
        jnp.where(delay == 4, far, 0.0),
    ]
    pieces = []
    for factor in factors:
        for _ in range(3):
            part = factor.astype(jnp.bfloat16).astype(jnp.float32)
            factor = factor - part
            pieces.append(part)
    spot = lax.broadcasted_iota(jnp.int32, (slots, LANES), 1)
    upper = jnp.zeros((slots, LANES), jnp.float32)
    lower = jnp.zeros((slots, LANES), jnp.float32)
    for index, piece in enumerate(pieces):
        if index < 8:
            upper = jnp.where(spot == index, piece, upper)
        else:
            lower = jnp.where(spot == index - 8, piece, lower)
    eye = jnp.where(
        lax.broadcasted_iota(jnp.int32, (8, LANES), 0) == lax.broadcasted_iota(jnp.int32, (8, LANES), 1), 1.0, 0.0
    ).astype(jnp.bfloat16)
    table = dot(eye, jnp.concatenate([upper, lower], axis=0).astype(jnp.bfloat16), NT)
    stack = jnp.concatenate([recv_hot, driving], axis=0)
    for load in wide:
        load.wait()
    picked = dot(stack, inverse_ref[...])
    lane = lax.broadcasted_iota(jnp.int32, picked.shape, 1)
    picked = jnp.where(lane < live, picked, 0.0).astype(jnp.bfloat16)
    rows = picked[:slots]
    rows_ref[...] = rows
    blank = jnp.zeros((columns, nodes), jnp.bfloat16)
    body = dot(send_hot, jnp.concatenate([picked, blank], axis=0), NT) + dot(
        rows, jnp.concatenate([blank] * (slots // columns + 1) + [fault_hot], axis=0), NT
    )
    found = jnp.concatenate([blank] * (slots // columns) + [picked[slots:] * fault_hot, blank], axis=0)
    last = jnp.where(lax.broadcasted_iota(jnp.int32, (8, nodes), 0) == 7, 1.0, 0.0).astype(jnp.bfloat16)
    table = table + dot(last, found, NT)
    message_ref[...] = jnp.concatenate([body, table], axis=0).astype(jnp.bfloat16)


def march_kernel(
    gathered_ref, spread_ref, rows_ref, first_hbm, fault_hbm, last_ref, first_ref, fault_ref, semaphores
):
    owners = gathered_ref.shape[0]
    slots = rows_ref.shape[0]
    columns = first_ref.shape[1]
    depth = slots // owners
    count = len(VARIANTS)
    place = owner_here()
    spots = held_spots(owners)

    def held_at(owner):
        apart = lax.bitwise_xor(jnp.int32(owner), place)
        spot = 0
        for bit in range(len(spots)):
            spot = lax.bitwise_xor(spot, ((apart >> bit) & 1) * spots[bit])
        return spot

    def exchange(parts):
        return [
            jnp.concatenate([part[depth * owner : depth * (owner + 1)] for part in parts], axis=0)
            for owner in range(owners)
        ]

    def rounded(value):
        return value.astype(jnp.bfloat16).astype(jnp.float32)

    def lanes(value, index):
        return value[:, LANES * index : LANES * (index + 1)]

    places = [held_at(owner) for owner in range(owners)]
    blocks = [gathered_ref[spot, :slots, :] for spot in places]
    tables = jnp.concatenate([gathered_ref[spot, slots:, :].astype(jnp.float32) for spot in places], axis=0)
    turned = jnp.concatenate([tables, tables], axis=0).T
    lane = lax.broadcasted_iota(jnp.int32, (slots, LANES), 1)
    turned = jnp.where(lane < LANES // 2, turned[:slots], turned[slots:])
    owner_lane = lane % (LANES // 2) // 8
    pieces = [jnp.where(owner_lane == o, turned, 0.0).astype(jnp.bfloat16) for o in range(owners)]
    factor = [dot(piece, spread_ref[:, : LANES * count]) for piece in pieces]
    factor = [[lanes(part, v) for part in factor] for v in range(count)]
    repeated = [dot(block, spread_ref[:, LANES * count :]) for block in blocks]
    seven = exchange([lanes(part, 0) for part in repeated])
    fault = [lanes(part, 1) for part in repeated]
    system = [block[:, :slots] for block in blocks]

    def seen(drive):
        total = fault[0] * drive[0].astype(jnp.float32)
        for o in range(1, owners):
            total = total + fault[o] * drive[o].astype(jnp.float32)
        return rounded(jnp.sum(total, axis=0, keepdims=True))

    near = [(factor[0][o] * seven[o]).astype(jnp.bfloat16) for o in range(owners)]
    wide = [(factor[1][o] * seven[o]).astype(jnp.bfloat16) for o in range(owners)]
    result = [dot(system[o], jnp.concatenate([near[o], wide[o]], axis=1)) for o in range(owners)]
    row_a = seen(near)
    arrived = exchange([rounded(part) for part in result])
    drive = [
        factor[2][o] * seven[o] + factor[3][o] * lanes(arrived[o], 0) + factor[4][o] * lanes(arrived[o], 1)
        for o in range(owners)
    ]
    drive = [part.astype(jnp.bfloat16) for part in drive]
    later = [factor[5][o] * lanes(arrived[o], 1) for o in range(owners)]
    result = [dot(system[o], drive[o]) for o in range(owners)]
    row_b = seen(drive)
    arrived = exchange([rounded(part) for part in result])
    later = [later[o] + factor[1][o] * arrived[o] for o in range(owners)]
    drive = [part + pltpu.roll(part, 2 * columns, 1) for part in later]
    for o in range(owners):
        last_ref[o] = drive[o]
    own = last_ref[place].T[columns : 2 * columns].astype(jnp.bfloat16)
    first_ref[0] = dot(own, rows_ref[...]).astype(jnp.bfloat16)
    save_first = pltpu.make_async_copy(first_ref, first_hbm, semaphores.at[0])
    save_first.start()
    row_c = seen([part.astype(jnp.bfloat16) for part in drive])
    row_s = sum(tables[8 * o + 7 : 8 * o + 8] for o in range(owners))

    def back(value, quarters):
        return pltpu.roll(value, LANES - quarters * columns, 1)

    table = [
        back(row_c, 1),
        row_c,
        back(row_b, 1),
        row_b,
        back(row_a, 1),
        row_a,
        jnp.zeros_like(row_a),
        back(row_s, 2),
    ]
    step = lax.broadcasted_iota(jnp.int32, (STEPS, LANES), 0)
    total = jnp.zeros((STEPS, LANES), jnp.float32)
    for index, value in enumerate(table):
        total = jnp.where(step == index, jnp.broadcast_to(value, total.shape), total)
    fault_ref[...] = total[:, :columns]
    save_fault = pltpu.make_async_copy(fault_ref, fault_hbm, semaphores.at[1])
    save_fault.start()
    save_first.wait()
    save_fault.wait()


def gathered_plan(
    inverses, cotangent, subnet_sizes, slot_into, slot_from, offsets, weights, admittance, fault_bus
):
    _, columns, nodes = cotangent.shape
    owners, depth = slot_into.shape[1:]
    slots = owners * depth
    height = slots + 8
    vmem = pl.BlockSpec(memory_space=pltpu.VMEM)
    hbm = pl.BlockSpec(memory_space=pltpu.HBM)
    arrays = (
        subnet_sizes[None], inverses, cotangent, slot_into, slot_from, offsets, weights, admittance, fault_bus[None],
    )
    message, rows = pl.pallas_call(
        pick_kernel,
        out_shape=(
            jax.ShapeDtypeStruct((height, LANES), jnp.bfloat16),
            jax.ShapeDtypeStruct((slots, nodes), jnp.bfloat16),
        ),
        in_specs=[vmem] + [hbm] * (len(arrays) - 1),
        out_specs=(vmem, vmem),
        scratch_shapes=[
            pltpu.VMEM(array.shape[1:] if array is inverses else array.shape, array.dtype) for array in arrays[1:]
        ]
        + [pltpu.SemaphoreType.DMA((len(arrays) - 2 + BANDS,))],
        compiler_params=pltpu.CompilerParams(vmem_limit_bytes=VMEM_LIMIT),
        name="pick",
    )(arrays[0], *(pltpu.with_memory_space_constraint(array, pltpu.HBM) for array in arrays[1:]))
    held = message[None]
    for mask in exchange_masks(owners):
        other = lax.ppermute(held, OWNER_AXES, [(i, i ^ mask) for i in range(owners)])
        held = jnp.concatenate([held, other], axis=0)
    spread = jnp.asarray(spread_matrix(columns, owners), jnp.bfloat16)
    outputs = (
        jax.ShapeDtypeStruct((1, columns, nodes), jnp.bfloat16),
        jax.ShapeDtypeStruct((STEPS, columns), jnp.float32),
    )
    return pl.pallas_call(
        march_kernel,
        out_shape=outputs,
        in_specs=[vmem] * 3,
        out_specs=(hbm, hbm),
        scratch_shapes=[
            pltpu.VMEM((owners, slots, LANES), jnp.float32),
            *(pltpu.VMEM(output.shape, output.dtype) for output in outputs),
            pltpu.SemaphoreType.DMA((2,)),
        ],
        compiler_params=pltpu.CompilerParams(vmem_limit_bytes=VMEM_LIMIT),
        name="march",
    )(held, spread, rows)


def exchanged_plan(
    inverses, cotangent, subnet_sizes, slot_into, slot_from, offsets, weights, admittance, fault_bus
):
    block_count, column_count, node_count = cotangent.shape
    owner_count = lax.axis_size(OWNER_AXES)
    slot_depth = slot_into.shape[2]
    slot_count = owner_count * slot_depth
    local_span = block_count * node_count
    active = (jnp.arange(node_count, dtype=jnp.int32)[None, :] < subnet_sizes[:, None]).astype(
        jnp.float32
    )
    node_ids = jnp.arange(local_span, dtype=jnp.int32)[None, :]
    send_hot = (slot_into.reshape(slot_count)[:, None] == node_ids).astype(jnp.bfloat16)
    send_hot = send_hot.reshape(slot_count, block_count, node_count)
    from_local = slot_from.reshape(slot_count)
    is_used = (from_local >= 0).astype(jnp.float32)
    recv_hot = (
        (from_local[:, None] == node_ids)
        .astype(jnp.float32)
        .reshape(slot_count, block_count, node_count)
    )
    delay_steps = offsets.reshape(slot_count)
    fraction = weights.reshape(slot_count)
    conduct = admittance.reshape(slot_count) * is_used
    arrivals = {}
    results = {}
    for step_now in range(STEPS - 1, -1, -1):
        history = jnp.zeros((block_count, column_count, node_count), jnp.float32)
        terms = jnp.zeros((column_count, slot_count), jnp.float32)
        present = False
        for source_step in range(step_now + 2, min(step_now + 6, STEPS)):
            step_gap = source_step - step_now
            factor = conduct * (
                fraction * (delay_steps == step_gap).astype(jnp.float32)
                + (1.0 - fraction) * (delay_steps + 1 == step_gap).astype(jnp.float32)
            )
            terms = terms + factor[None, :] * arrivals[source_step].astype(jnp.float32)
            present = True
        if present:
            history = jnp.einsum("sk,kjn->jsn", terms, recv_hot, precision=lax.Precision.HIGHEST)
        if step_now == STEPS - 1:
            history = cotangent.astype(jnp.float32)
        driving = (history * active[:, None, :]).astype(jnp.bfloat16)
        adjoint = jnp.einsum("jsn,jnm->jsm", driving, inverses, preferred_element_type=jnp.float32)
        results[step_now] = (adjoint * active[:, None, :]).astype(jnp.bfloat16)
        if step_now >= 2:
            picked = jnp.einsum(
                "jsn,kjn->sk", results[step_now], send_hot, preferred_element_type=jnp.float32
            )
            arrivals[step_now] = lax.all_to_all(
                picked.astype(jnp.bfloat16)[None], OWNER_AXES, split_axis=2, concat_axis=2, tiled=True
            )[0]
    owner_index = lax.axis_index(OWNER_AXES)
    local_bus = fault_bus - owner_index * local_span
    owned = (local_bus >= 0) & (local_bus < local_span)
    clamped = jnp.clip(local_bus, 0, local_span - 1)
    position = (
        clamped // node_count * column_count * node_count
        + jnp.arange(column_count, dtype=jnp.int32) * node_count
        + clamped % node_count
    )
    sensitivity = jnp.stack(
        [
            jnp.where(
                owned, jnp.take(results[index].reshape(-1), position).astype(jnp.float32), 0.0
            )
            for index in range(STEPS)
        ]
    )
    return results[0], lax.psum(sensitivity, OWNER_AXES)


def per_device(*arrays):
    blocks, columns, nodes = arrays[1].shape
    owners, depth = arrays[3].shape[1:]
    slots = owners * depth
    fits = (
        blocks == 1
        and columns * 4 == LANES
        and depth == 8
        and owners & (owners - 1) == 0
        and slots + 2 * columns == LANES
        and nodes % LANES == 0
    )
    return gathered_plan(*arrays) if fits else exchanged_plan(*arrays)


def solution(mesh):
    return jax.shard_map(
        per_device,
        mesh=mesh,
        in_specs=(
            P(("groups", "sub", "half"), None, None),
            P(("groups", "sub", "half"), "scen", None),
            P(("groups", "sub", "half")),
            P(("groups", "sub", "half"), None, None),
            P(("groups", "sub", "half"), None, None),
            P(("groups", "sub", "half"), None, None),
            P(("groups", "sub", "half"), None, None),
            P(("groups", "sub", "half"), None, None),
            P(("groups", "scen")),
        ),
        out_specs=(P(("groups", "sub", "half"), "scen", None), P(None, ("groups", "scen"))),
        check_vma=False,
    )
```

```python
import jax
import jax.numpy as jnp
import numpy as np
from jax import lax
from jax.experimental import pallas as pl
from jax.experimental.pallas import tpu as pltpu
from jax.sharding import PartitionSpec as P

STEPS = 8
LANES = 128
VMEM_LIMIT = 16 * 2**20
HINT_FLOPS = 4 * 2**30
HINT_BYTES = 8 * 2**20
OWNER_AXES = ("sub", "half")
VARIANTS = (
    (2, 3, 0, 2),
    (2, 2, 3, 3),
    (4, 5, 0, 4),
    (2, 2, 0, 2),
    (0, 3, 0, 0),
    (4, 5, 3, 4),
)
NT = (((1,), (1,)), ((), ()))


def dot(left, right, dims=(((1,), (0,)), ((), ()))):
    return lax.dot_general(left, right, dims, preferred_element_type=jnp.float32)


def spread_matrix(column_count, owners):
    half = LANES // 2
    spread = np.zeros((LANES, (len(VARIANTS) + 2) * LANES), np.float32)
    for variant, gaps in enumerate(VARIANTS):
        for quarter, gap in enumerate(gaps):
            lane = variant * LANES + quarter * column_count
            for piece in range(3 * (gap - 2), 3 * (gap - 1)) if gap else ():
                for owner in range(owners):
                    spread[piece // 8 * half + owner * 8 + piece % 8, lane : lane + column_count] = 1
    for lane in range(LANES):
        for part in range(2):
            start = half + part * column_count
            spread[start + lane % column_count, (len(VARIANTS) + part) * LANES + lane] = 1
    return spread


def exchange_masks(owners):
    masks = []
    reach = owners // 2
    while reach > 1:
        masks.append(reach + 1)
        reach //= 2
    return masks + [1]


def held_order(owners):
    far, near, core = exchange_masks(owners)
    first = [0, far]
    later = [near, near ^ far]
    return first + [x ^ core for x in first] + later + [x ^ core for x in later]


def column_of(ref, place):
    _, peers, depth = ref.shape
    eye = lax.broadcasted_iota(jnp.int32, (depth, depth), 0) == lax.broadcasted_iota(
        jnp.int32, (depth, depth), 1
    )
    rows = [
        jnp.where(eye, jnp.broadcast_to(row.astype(jnp.float32), (depth, depth)), 0.0)
        for row in (ref[0, pl.ds(lax.bitwise_xor(place, jnp.int32(apart)), 1), :] for apart in range(peers))
    ]
    return jnp.sum(jnp.concatenate(rows, axis=0), axis=1, keepdims=True)


def owner_here():
    return lax.axis_index(OWNER_AXES[0]) * lax.axis_size(OWNER_AXES[1]) + lax.axis_index(OWNER_AXES[1])


def lane_kernel(lane_ref):
    lane_ref[...] = lax.broadcasted_iota(jnp.int32, lane_ref.shape, 1).astype(jnp.float32)


def pick_kernel(
    size_ref, lane_ref, into_ref, from_ref, offset_ref, weight_ref, admit_ref, bus_ref, inverse_ref, cotangent_ref,
    message_ref, rows_ref,
):
    nodes = inverse_ref.shape[1]
    _, peers, depth = into_ref.shape
    slots = peers * depth
    columns = cotangent_ref.shape[1]
    lane_f = jnp.broadcast_to(lane_ref[:1], (slots, nodes))
    live = size_ref[0]
    alive = lane_f < live.astype(jnp.float32)
    place = owner_here()
    into = column_of(into_ref, place)
    source = column_of(from_ref, place)
    delay = column_of(offset_ref, place)
    weight = column_of(weight_ref, place)
    admit = column_of(admit_ref, place)
    recv_hot = jnp.where((source == lane_f) & alive, 1.0, 0.0).astype(jnp.bfloat16)
    send_hot = jnp.where(into == lane_f, 1.0, 0.0).astype(jnp.bfloat16)
    driving = jnp.where(alive[:columns], cotangent_ref[0].astype(jnp.float32), 0.0).astype(jnp.bfloat16)
    bus = (bus_ref[...] - place * nodes).astype(jnp.float32)
    eye = lax.broadcasted_iota(jnp.int32, (columns, columns), 0) == lax.broadcasted_iota(
        jnp.int32, (columns, columns), 1
    )
    bus = jnp.sum(jnp.where(eye, jnp.broadcast_to(bus, (columns, columns)), 0.0), axis=1, keepdims=True)
    fault_hot = jnp.where(bus == lane_f[:columns], 1.0, 0.0).astype(jnp.bfloat16)
    conduct = jnp.where(source >= 0, admit, 0.0)
    near, far = conduct * weight, conduct * (1.0 - weight)
    factors = [
        jnp.where(delay == 2, near, 0.0),
        jnp.where(delay == 3, near, 0.0) + jnp.where(delay == 2, far, 0.0),
        jnp.where(delay == 4, near, 0.0) + jnp.where(delay == 3, far, 0.0),
        jnp.where(delay == 4, far, 0.0),
    ]
    pieces = []
    for factor in factors:
        for _ in range(3):
            part = factor.astype(jnp.bfloat16).astype(jnp.float32)
            factor = factor - part
            pieces.append(part)
    spot = lax.broadcasted_iota(jnp.int32, (slots, LANES), 1)
    upper = jnp.zeros((slots, LANES), jnp.float32)
    lower = jnp.zeros((slots, LANES), jnp.float32)
    for index, piece in enumerate(pieces):
        if index < 8:
            upper = jnp.where(spot == index, piece, upper)
        else:
            lower = jnp.where(spot == index - 8, piece, lower)
    eye = jnp.where(
        lax.broadcasted_iota(jnp.int32, (8, LANES), 0) == lax.broadcasted_iota(jnp.int32, (8, LANES), 1), 1.0, 0.0
    ).astype(jnp.bfloat16)
    table = dot(eye, jnp.concatenate([upper, lower], axis=0).astype(jnp.bfloat16), NT)
    stack = jnp.concatenate([recv_hot, driving], axis=0)
    picked = dot(stack, inverse_ref[0])
    lane = lax.broadcasted_iota(jnp.int32, picked.shape, 1)
    picked = jnp.where(lane < live, picked, 0.0).astype(jnp.bfloat16)
    rows = picked[:slots]
    rows_ref[...] = rows
    blank = jnp.zeros((columns, nodes), jnp.bfloat16)
    body = dot(send_hot, jnp.concatenate([picked, blank], axis=0), NT) + dot(
        rows, jnp.concatenate([blank] * (slots // columns + 1) + [fault_hot], axis=0), NT
    )
    found = jnp.concatenate([blank] * (slots // columns) + [picked[slots:] * fault_hot, blank], axis=0)
    last = jnp.where(lax.broadcasted_iota(jnp.int32, (8, nodes), 0) == 7, 1.0, 0.0).astype(jnp.bfloat16)
    table = table + dot(last, found, NT)
    message_ref[...] = jnp.concatenate([body, table], axis=0).astype(jnp.bfloat16)


def lanes(value, index):
    return value[:, LANES * index : LANES * (index + 1)]


def turned_pieces(messages):
    slots = LANES // 2
    tables = [message[slots:].astype(jnp.float32) for message in messages]
    filled = tables + [jnp.zeros((8, LANES), jnp.float32)] * (8 - len(tables))
    turned = jnp.concatenate(filled * 2, axis=0).T
    lane = lax.broadcasted_iota(jnp.int32, (slots, LANES), 1)
    turned = jnp.where(lane < LANES // 2, turned[:slots], turned[slots:])
    group = lane % (LANES // 2) // 8
    return [jnp.where(group == index, turned, 0.0).astype(jnp.bfloat16) for index in range(len(messages))]


def widen_kernel(*refs):
    *held_refs, spread_ref, wide_ref = refs
    messages = [ref[p] for ref in held_refs for p in range(ref.shape[0])]
    count = LANES * len(VARIANTS)
    for index, piece in enumerate(turned_pieces(messages)):
        wide_ref[index, :, :count] = dot(piece, spread_ref[:, :count])
        wide_ref[index, :, count:] = dot(messages[index][: LANES // 2], spread_ref[:, count:])


def march_kernel(
    first_pair, first_other, later_pair, later_other, first_wide, later_wide, spread_ref, rows_ref,
    first_hbm, fault_hbm, first_ref, fault_ref, semaphores,
):
    held = (first_pair, first_other, later_pair, later_other)
    owners = sum(ref.shape[0] for ref in held)
    slots = rows_ref.shape[0]
    columns = first_ref.shape[1]
    depth = slots // owners
    count = len(VARIANTS)
    order = held_order(owners)
    spot = {apart: index for index, apart in enumerate(order)}

    def exchange(parts):
        return [
            jnp.concatenate(
                [parts[spot[mine ^ other]][depth * other : depth * (other + 1)] for other in range(owners)], axis=0
            )
            for mine in order
        ]

    def rounded(value):
        return value.astype(jnp.bfloat16).astype(jnp.float32)

    blocks = [ref[p] for ref in held for p in range(ref.shape[0])]
    system = [block[:slots, :slots] for block in blocks]
    fresh = blocks[-later_other.shape[0] :]
    pieces = turned_pieces(fresh)

    def spread_of(index, sources):
        pair = slice(LANES * index, LANES * (index + 2))
        known = [ref[p, :, pair] for ref in (first_wide, later_wide) for p in range(ref.shape[0])]
        both = known + [dot(source, spread_ref[:, pair]) for source in sources]
        return [lanes(part, 0) for part in both], [lanes(part, 1) for part in both]

    seven, fault = spread_of(count, [block[:slots] for block in fresh])
    seven = exchange(seven)
    factor = [*spread_of(0, pieces)]

    def seen(drive):
        total = fault[0] * drive[0].astype(jnp.float32)
        for o in range(1, owners):
            total = total + fault[o] * drive[o].astype(jnp.float32)
        return rounded(jnp.sum(total, axis=0, keepdims=True))

    near = [(factor[0][o] * seven[o]).astype(jnp.bfloat16) for o in range(owners)]
    wide = [(factor[1][o] * seven[o]).astype(jnp.bfloat16) for o in range(owners)]
    result = [dot(system[o], jnp.concatenate([near[o], wide[o]], axis=1)) for o in range(owners)]
    factor += [*spread_of(2, pieces), *spread_of(4, pieces)]
    row_a = seen(near)
    arrived = exchange([rounded(part) for part in result])
    drive = [
        factor[2][o] * seven[o] + factor[3][o] * lanes(arrived[o], 0) + factor[4][o] * lanes(arrived[o], 1)
        for o in range(owners)
    ]
    drive = [part.astype(jnp.bfloat16) for part in drive]
    later = [factor[5][o] * lanes(arrived[o], 1) for o in range(owners)]
    result = [dot(system[o], drive[o]) for o in range(owners)]
    row_b = seen(drive)
    arrived = exchange([rounded(part) for part in result])
    later = [later[o] + factor[1][o] * arrived[o] for o in range(owners)]
    drive = [part + pltpu.roll(part, 2 * columns, 1) for part in later]
    own = drive[0].T[columns : 2 * columns].astype(jnp.bfloat16)
    first_ref[0] = dot(own, rows_ref[...]).astype(jnp.bfloat16)
    save_first = pltpu.make_async_copy(first_ref, first_hbm, semaphores.at[0])
    save_first.start()
    row_c = seen([part.astype(jnp.bfloat16) for part in drive])
    row_s = sum(block[slots + 7 : slots + 8].astype(jnp.float32) for block in blocks)

    def back(value, quarters):
        return pltpu.roll(value, LANES - quarters * columns, 1)

    table = [
        back(row_c, 1),
        row_c,
        back(row_b, 1),
        row_b,
        back(row_a, 1),
        row_a,
        jnp.zeros_like(row_a),
        back(row_s, 2),
    ]
    step = lax.broadcasted_iota(jnp.int32, (STEPS, LANES), 0)
    total = jnp.zeros((STEPS, LANES), jnp.float32)
    for index, value in enumerate(table):
        total = jnp.where(step == index, jnp.broadcast_to(value, total.shape), total)
    fault_ref[...] = total[:, :columns]
    save_fault = pltpu.make_async_copy(fault_ref, fault_hbm, semaphores.at[1])
    save_fault.start()
    save_first.wait()
    save_fault.wait()


def gathered_plan(
    inverses, cotangent, subnet_sizes, slot_into, slot_from, offsets, weights, admittance, fault_bus
):
    _, columns, nodes = cotangent.shape
    owners, depth = slot_into.shape[1:]
    slots = owners * depth
    height = slots + 8
    vmem = pl.BlockSpec(memory_space=pltpu.VMEM)
    hbm = pl.BlockSpec(memory_space=pltpu.HBM)
    smem = pl.BlockSpec(memory_space=pltpu.SMEM)
    lane = pl.pallas_call(
        lane_kernel,
        out_shape=jax.ShapeDtypeStruct((8, nodes), jnp.float32),
        out_specs=vmem,
        compiler_params=pltpu.CompilerParams(vmem_limit_bytes=VMEM_LIMIT),
        cost_estimate=pl.CostEstimate(flops=HINT_FLOPS, bytes_accessed=HINT_BYTES, transcendentals=0),
        name="lane",
    )()
    lane, sizes = lax.optimization_barrier((lane, subnet_sizes))
    arrays = (
        sizes, lane, slot_into, slot_from, offsets, weights, admittance, fault_bus[None], inverses, cotangent,
    )
    message, rows = pl.pallas_call(
        pick_kernel,
        out_shape=(
            jax.ShapeDtypeStruct((height, LANES), jnp.bfloat16),
            jax.ShapeDtypeStruct((slots, nodes), jnp.bfloat16),
        ),
        in_specs=[smem] + [vmem] * (len(arrays) - 1),
        out_specs=(vmem, vmem),
        compiler_params=pltpu.CompilerParams(vmem_limit_bytes=VMEM_LIMIT),
        name="pick",
    )(*arrays)
    spread = jnp.asarray(spread_matrix(columns, 8), jnp.bfloat16)
    width = spread.shape[1]

    def swap(held, mask):
        return lax.ppermute(held, OWNER_AXES, [(i, i ^ mask) for i in range(owners)])

    def widen(*held):
        count = sum(part.shape[0] for part in held)
        return pl.pallas_call(
            widen_kernel,
            out_shape=jax.ShapeDtypeStruct((count, slots, width), jnp.float32),
            in_specs=[vmem] * (len(held) + 1),
            out_specs=vmem,
            compiler_params=pltpu.CompilerParams(vmem_limit_bytes=VMEM_LIMIT),
            cost_estimate=pl.CostEstimate(
                flops=2 * count * slots * LANES * width, bytes_accessed=4 * count * slots * width, transcendentals=0
            ),
            name="widen",
        )(*held, spread)

    far, near, core = exchange_masks(owners)
    first = jnp.concatenate([message[None], swap(message[None], far)], axis=0)
    later = swap(first, near)
    first_other = swap(first, core)
    first_wide = widen(first, first_other)
    later_other = swap(later, core)
    later_wide = widen(later)
    outputs = (
        jax.ShapeDtypeStruct((1, columns, nodes), jnp.bfloat16),
        jax.ShapeDtypeStruct((STEPS, columns), jnp.float32),
    )
    return pl.pallas_call(
        march_kernel,
        out_shape=outputs,
        in_specs=[vmem] * 8,
        out_specs=(hbm, hbm),
        scratch_shapes=[
            *(pltpu.VMEM(output.shape, output.dtype) for output in outputs),
            pltpu.SemaphoreType.DMA((2,)),
        ],
        compiler_params=pltpu.CompilerParams(vmem_limit_bytes=VMEM_LIMIT),
        name="march",
    )(first, first_other, later, later_other, first_wide, later_wide, spread, rows)


def exchanged_plan(
    inverses, cotangent, subnet_sizes, slot_into, slot_from, offsets, weights, admittance, fault_bus
):
    block_count, column_count, node_count = cotangent.shape
    owner_count = lax.axis_size(OWNER_AXES)
    slot_depth = slot_into.shape[2]
    slot_count = owner_count * slot_depth
    local_span = block_count * node_count
    active = (jnp.arange(node_count, dtype=jnp.int32)[None, :] < subnet_sizes[:, None]).astype(
        jnp.float32
    )
    node_ids = jnp.arange(local_span, dtype=jnp.int32)[None, :]
    send_hot = (slot_into.reshape(slot_count)[:, None] == node_ids).astype(jnp.bfloat16)
    send_hot = send_hot.reshape(slot_count, block_count, node_count)
    from_local = slot_from.reshape(slot_count)
    is_used = (from_local >= 0).astype(jnp.float32)
    recv_hot = (
        (from_local[:, None] == node_ids)
        .astype(jnp.float32)
        .reshape(slot_count, block_count, node_count)
    )
    delay_steps = offsets.reshape(slot_count)
    fraction = weights.reshape(slot_count)
    conduct = admittance.reshape(slot_count) * is_used
    arrivals = {}
    results = {}
    for step_now in range(STEPS - 1, -1, -1):
        history = jnp.zeros((block_count, column_count, node_count), jnp.float32)
        terms = jnp.zeros((column_count, slot_count), jnp.float32)
        present = False
        for source_step in range(step_now + 2, min(step_now + 6, STEPS)):
            step_gap = source_step - step_now
            factor = conduct * (
                fraction * (delay_steps == step_gap).astype(jnp.float32)
                + (1.0 - fraction) * (delay_steps + 1 == step_gap).astype(jnp.float32)
            )
            terms = terms + factor[None, :] * arrivals[source_step].astype(jnp.float32)
            present = True
        if present:
            history = jnp.einsum("sk,kjn->jsn", terms, recv_hot, precision=lax.Precision.HIGHEST)
        if step_now == STEPS - 1:
            history = cotangent.astype(jnp.float32)
        driving = (history * active[:, None, :]).astype(jnp.bfloat16)
        adjoint = jnp.einsum("jsn,jnm->jsm", driving, inverses, preferred_element_type=jnp.float32)
        results[step_now] = (adjoint * active[:, None, :]).astype(jnp.bfloat16)
        if step_now >= 2:
            picked = jnp.einsum(
                "jsn,kjn->sk", results[step_now], send_hot, preferred_element_type=jnp.float32
            )
            arrivals[step_now] = lax.all_to_all(
                picked.astype(jnp.bfloat16)[None], OWNER_AXES, split_axis=2, concat_axis=2, tiled=True
            )[0]
    owner_index = lax.axis_index(OWNER_AXES)
    local_bus = fault_bus - owner_index * local_span
    owned = (local_bus >= 0) & (local_bus < local_span)
    clamped = jnp.clip(local_bus, 0, local_span - 1)
    position = (
        clamped // node_count * column_count * node_count
        + jnp.arange(column_count, dtype=jnp.int32) * node_count
        + clamped % node_count
    )
    sensitivity = jnp.stack(
        [
            jnp.where(
                owned, jnp.take(results[index].reshape(-1), position).astype(jnp.float32), 0.0
            )
            for index in range(STEPS)
        ]
    )
    return results[0], lax.psum(sensitivity, OWNER_AXES)


def per_device(*arrays):
    blocks, columns, nodes = arrays[1].shape
    owners, depth = arrays[3].shape[1:]
    slots = owners * depth
    fits = (
        blocks == 1
        and columns * 4 == LANES
        and depth == 8
        and owners == 8
        and slots + 2 * columns == LANES
        and nodes % LANES == 0
    )
    return gathered_plan(*arrays) if fits else exchanged_plan(*arrays)


def solution(mesh):
    return jax.shard_map(
        per_device,
        mesh=mesh,
        in_specs=(
            P(("groups", "sub", "half"), None, None),
            P(("groups", "sub", "half"), "scen", None),
            P(("groups", "sub", "half")),
            P(("groups", "sub", "half"), None, None),
            P(("groups", "sub", "half"), None, None),
            P(("groups", "sub", "half"), None, None),
            P(("groups", "sub", "half"), None, None),
            P(("groups", "sub", "half"), None, None),
            P(("groups", "scen")),
        ),
        out_specs=(P(("groups", "sub", "half"), "scen", None), P(None, ("groups", "scen"))),
        check_vma=False,
    )
```

```python
import jax
import jax.numpy as jnp
import numpy as np
from jax import lax
from jax.experimental import pallas as pl
from jax.experimental.pallas import tpu as pltpu
from jax.sharding import PartitionSpec as P

STEPS = 8
LANES = 128
VMEM_LIMIT = 16 * 2**20
HINT_FLOPS = 4 * 2**30
HINT_BYTES = 8 * 2**20
OWNER_AXES = ("sub", "half")
VARIANTS = (
    (2, 3, 0, 2),
    (2, 2, 3, 3),
    (4, 5, 0, 4),
    (2, 2, 0, 2),
    (0, 3, 0, 0),
    (4, 5, 3, 4),
)
NT = (((1,), (1,)), ((), ()))


def dot(left, right, dims=(((1,), (0,)), ((), ()))):
    return lax.dot_general(left, right, dims, preferred_element_type=jnp.float32)


def spread_matrix(column_count, owners):
    half = LANES // 2
    spread = np.zeros((LANES, (len(VARIANTS) + 2) * LANES), np.float32)
    for variant, gaps in enumerate(VARIANTS):
        for quarter, gap in enumerate(gaps):
            lane = variant * LANES + quarter * column_count
            for piece in range(3 * (gap - 2), 3 * (gap - 1)) if gap else ():
                for owner in range(owners):
                    spread[piece // 8 * half + owner * 8 + piece % 8, lane : lane + column_count] = 1
    for lane in range(LANES):
        for part in range(2):
            start = half + part * column_count
            spread[start + lane % column_count, (len(VARIANTS) + part) * LANES + lane] = 1
    return spread


SOURCES = ((1, 0, 3, 2), (2, 3, 1, 0), (3, 2, 0, 1))
HELD = (0, 3, 5, 7, 1, 2, 4, 6)


def column_of(ref, place):
    _, peers, depth = ref.shape
    eye = lax.broadcasted_iota(jnp.int32, (depth, depth), 0) == lax.broadcasted_iota(
        jnp.int32, (depth, depth), 1
    )
    rows = [
        jnp.where(eye, jnp.broadcast_to(row.astype(jnp.float32), (depth, depth)), 0.0)
        for row in (ref[0, pl.ds(lax.bitwise_xor(place, jnp.int32(apart)), 1), :] for apart in range(peers))
    ]
    return jnp.sum(jnp.concatenate(rows, axis=0), axis=1, keepdims=True)


def owner_here():
    return lax.axis_index(OWNER_AXES[0]) * lax.axis_size(OWNER_AXES[1]) + lax.axis_index(OWNER_AXES[1])


def lane_kernel(lane_ref):
    lane_ref[...] = lax.broadcasted_iota(jnp.int32, lane_ref.shape, 1).astype(jnp.float32)


def pick_kernel(
    size_ref, lane_ref, into_ref, from_ref, offset_ref, weight_ref, admit_ref, bus_ref, inverse_ref, cotangent_ref,
    message_ref, rows_ref,
):
    nodes = inverse_ref.shape[1]
    _, peers, depth = into_ref.shape
    slots = peers * depth
    columns = cotangent_ref.shape[1]
    lane_f = jnp.broadcast_to(lane_ref[:1], (slots, nodes))
    live = size_ref[0]
    alive = lane_f < live.astype(jnp.float32)
    place = owner_here()
    into = column_of(into_ref, place)
    source = column_of(from_ref, place)
    recv_hot = jnp.where((source == lane_f) & alive, 1.0, 0.0).astype(jnp.bfloat16)
    send_hot = jnp.where(into == lane_f, 1.0, 0.0).astype(jnp.bfloat16)
    driving = jnp.where(alive[:columns], cotangent_ref[0].astype(jnp.float32), 0.0).astype(jnp.bfloat16)
    stack = jnp.concatenate([recv_hot, driving], axis=0)
    picked = dot(stack, inverse_ref[0])
    lane = lax.broadcasted_iota(jnp.int32, picked.shape, 1)
    picked = jnp.where(lane < live, picked, 0.0).astype(jnp.bfloat16)
    bus = (bus_ref[...] - place * nodes).astype(jnp.float32)
    eye = lax.broadcasted_iota(jnp.int32, (columns, columns), 0) == lax.broadcasted_iota(
        jnp.int32, (columns, columns), 1
    )
    bus = jnp.sum(jnp.where(eye, jnp.broadcast_to(bus, (columns, columns)), 0.0), axis=1, keepdims=True)
    fault_hot = jnp.where(bus == lane_f[:columns], 1.0, 0.0).astype(jnp.bfloat16)
    delay = column_of(offset_ref, place)
    weight = column_of(weight_ref, place)
    admit = column_of(admit_ref, place)
    conduct = jnp.where(source >= 0, admit, 0.0)
    near, far = conduct * weight, conduct * (1.0 - weight)
    factors = [
        jnp.where(delay == 2, near, 0.0),
        jnp.where(delay == 3, near, 0.0) + jnp.where(delay == 2, far, 0.0),
        jnp.where(delay == 4, near, 0.0) + jnp.where(delay == 3, far, 0.0),
        jnp.where(delay == 4, far, 0.0),
    ]
    pieces = []
    for factor in factors:
        for _ in range(3):
            part = factor.astype(jnp.bfloat16).astype(jnp.float32)
            factor = factor - part
            pieces.append(part)
    spot = lax.broadcasted_iota(jnp.int32, (slots, LANES), 1)
    upper = jnp.zeros((slots, LANES), jnp.float32)
    lower = jnp.zeros((slots, LANES), jnp.float32)
    for index, piece in enumerate(pieces):
        if index < 8:
            upper = jnp.where(spot == index, piece, upper)
        else:
            lower = jnp.where(spot == index - 8, piece, lower)
    eye = jnp.where(
        lax.broadcasted_iota(jnp.int32, (8, LANES), 0) == lax.broadcasted_iota(jnp.int32, (8, LANES), 1), 1.0, 0.0
    ).astype(jnp.bfloat16)
    table = dot(eye, jnp.concatenate([upper, lower], axis=0).astype(jnp.bfloat16), NT)
    rows = picked[:slots]
    rows_ref[...] = rows
    blank = jnp.zeros((columns, nodes), jnp.bfloat16)
    body = dot(send_hot, jnp.concatenate([picked, blank], axis=0), NT) + dot(
        rows, jnp.concatenate([blank] * (slots // columns + 1) + [fault_hot], axis=0), NT
    )
    found = jnp.concatenate([blank] * (slots // columns) + [picked[slots:] * fault_hot, blank], axis=0)
    last = jnp.where(lax.broadcasted_iota(jnp.int32, (8, nodes), 0) == 7, 1.0, 0.0).astype(jnp.bfloat16)
    table = table + dot(last, found, NT)
    message_ref[...] = jnp.concatenate([body, table], axis=0).astype(jnp.bfloat16)


def lanes(value, index):
    return value[:, LANES * index : LANES * (index + 1)]


def turned_pieces(messages):
    slots = LANES // 2
    tables = [message[slots:].astype(jnp.float32) for message in messages]
    filled = tables + [jnp.zeros((8, LANES), jnp.float32)] * (8 - len(tables))
    turned = jnp.concatenate(filled * 2, axis=0).T
    lane = lax.broadcasted_iota(jnp.int32, (slots, LANES), 1)
    turned = jnp.where(lane < LANES // 2, turned[:slots], turned[slots:])
    group = lane % (LANES // 2) // 8
    return [jnp.where(group == index, turned, 0.0).astype(jnp.bfloat16) for index in range(len(messages))]


def widen_kernel(near_ref, spread_ref, wide_ref):
    messages = [near_ref[p] for p in range(near_ref.shape[0])]
    count = LANES * len(VARIANTS)
    for index, piece in enumerate(turned_pieces(messages)):
        wide_ref[index, :, :count] = dot(piece, spread_ref[:, :count])
        wide_ref[index, :, count:] = dot(messages[index][: LANES // 2], spread_ref[:, count:])


def march_kernel(
    near_ref, far_ref, wide_ref, spread_ref, rows_ref, first_hbm, fault_hbm, first_ref, fault_ref, semaphores
):
    held = (near_ref, far_ref)
    owners = sum(ref.shape[0] for ref in held)
    slots = rows_ref.shape[0]
    columns = first_ref.shape[1]
    depth = slots // owners
    count = len(VARIANTS)
    order = HELD
    spot = {apart: index for index, apart in enumerate(order)}

    def exchange(parts):
        return [
            jnp.concatenate(
                [parts[spot[mine ^ other]][depth * other : depth * (other + 1)] for other in range(owners)], axis=0
            )
            for mine in order
        ]

    def rounded(value):
        return value.astype(jnp.bfloat16).astype(jnp.float32)

    blocks = [ref[p] for ref in held for p in range(ref.shape[0])]
    system = [block[:slots, :slots] for block in blocks]
    fresh = blocks[-far_ref.shape[0] :]
    pieces = turned_pieces(fresh)

    def spread_of(index, sources):
        pair = slice(LANES * index, LANES * (index + 2))
        known = [wide_ref[p, :, pair] for p in range(wide_ref.shape[0])]
        both = known + [dot(source, spread_ref[:, pair]) for source in sources]
        return [lanes(part, 0) for part in both], [lanes(part, 1) for part in both]

    seven, fault = spread_of(count, [block[:slots] for block in fresh])
    seven = exchange(seven)
    factor = [*spread_of(0, pieces)]

    def seen(drive):
        total = fault[0] * drive[0].astype(jnp.float32)
        for o in range(1, owners):
            total = total + fault[o] * drive[o].astype(jnp.float32)
        return rounded(jnp.sum(total, axis=0, keepdims=True))

    near = [(factor[0][o] * seven[o]).astype(jnp.bfloat16) for o in range(owners)]
    wide = [(factor[1][o] * seven[o]).astype(jnp.bfloat16) for o in range(owners)]
    result = [dot(system[o], jnp.concatenate([near[o], wide[o]], axis=1)) for o in range(owners)]
    factor += [*spread_of(2, pieces), *spread_of(4, pieces)]
    row_a = seen(near)
    arrived = exchange([rounded(part) for part in result])
    drive = [
        factor[2][o] * seven[o] + factor[3][o] * lanes(arrived[o], 0) + factor[4][o] * lanes(arrived[o], 1)
        for o in range(owners)
    ]
    drive = [part.astype(jnp.bfloat16) for part in drive]
    later = [factor[5][o] * lanes(arrived[o], 1) for o in range(owners)]
    result = [dot(system[o], drive[o]) for o in range(owners)]
    row_b = seen(drive)
    arrived = exchange([rounded(part) for part in result])
    later = [later[o] + factor[1][o] * arrived[o] for o in range(owners)]
    drive = [part + pltpu.roll(part, 2 * columns, 1) for part in later]
    own = drive[0].T[columns : 2 * columns].astype(jnp.bfloat16)
    first_ref[0] = dot(own, rows_ref[...]).astype(jnp.bfloat16)
    save_first = pltpu.make_async_copy(first_ref, first_hbm, semaphores.at[0])
    save_first.start()
    row_c = seen([part.astype(jnp.bfloat16) for part in drive])
    row_s = sum(block[slots + 7 : slots + 8].astype(jnp.float32) for block in blocks)

    def back(value, quarters):
        return pltpu.roll(value, LANES - quarters * columns, 1)

    table = [
        back(row_c, 1),
        row_c,
        back(row_b, 1),
        row_b,
        back(row_a, 1),
        row_a,
        jnp.zeros_like(row_a),
        back(row_s, 2),
    ]
    step = lax.broadcasted_iota(jnp.int32, (STEPS, LANES), 0)
    total = jnp.zeros((STEPS, LANES), jnp.float32)
    for index, value in enumerate(table):
        total = jnp.where(step == index, jnp.broadcast_to(value, total.shape), total)
    fault_ref[...] = total[:, :columns]
    save_fault = pltpu.make_async_copy(fault_ref, fault_hbm, semaphores.at[1])
    save_fault.start()
    save_first.wait()
    save_fault.wait()


def gathered_plan(
    inverses, cotangent, subnet_sizes, slot_into, slot_from, offsets, weights, admittance, fault_bus
):
    _, columns, nodes = cotangent.shape
    owners, depth = slot_into.shape[1:]
    slots = owners * depth
    height = slots + 8
    vmem = pl.BlockSpec(memory_space=pltpu.VMEM)
    hbm = pl.BlockSpec(memory_space=pltpu.HBM)
    smem = pl.BlockSpec(memory_space=pltpu.SMEM)
    lane = pl.pallas_call(
        lane_kernel,
        out_shape=jax.ShapeDtypeStruct((8, nodes), jnp.float32),
        out_specs=vmem,
        compiler_params=pltpu.CompilerParams(vmem_limit_bytes=VMEM_LIMIT),
        cost_estimate=pl.CostEstimate(flops=HINT_FLOPS, bytes_accessed=HINT_BYTES, transcendentals=0),
        name="lane",
    )()
    lane, sizes = lax.optimization_barrier((lane, subnet_sizes))
    arrays = (
        sizes, lane, slot_into, slot_from, offsets, weights, admittance, fault_bus[None], inverses, cotangent,
    )
    message, rows = pl.pallas_call(
        pick_kernel,
        out_shape=(
            jax.ShapeDtypeStruct((height, LANES), jnp.bfloat16),
            jax.ShapeDtypeStruct((slots, nodes), jnp.bfloat16),
        ),
        in_specs=[smem] + [vmem] * (len(arrays) - 1),
        out_specs=(vmem, vmem),
        compiler_params=pltpu.CompilerParams(vmem_limit_bytes=VMEM_LIMIT),
        name="pick",
    )(*arrays)
    spread = jnp.asarray(spread_matrix(columns, 8), jnp.bfloat16)
    width = spread.shape[1]


    def send(held, sources):
        pairs = [(2 * source + core, 2 * z + 1 - core) for z, source in enumerate(sources) for core in range(2)]
        return lax.ppermute(held, OWNER_AXES, pairs)

    own = message[None]
    beside, second, third = (send(own, sources) for sources in SOURCES)
    low = lax.axis_index(OWNER_AXES[0]) < 2
    near = jnp.concatenate([own, beside, jnp.where(low, second, third), jnp.where(low, third, second)], axis=0)
    far = send(near, range(len(SOURCES) + 1))
    wide = pl.pallas_call(
        widen_kernel,
        out_shape=jax.ShapeDtypeStruct((near.shape[0], slots, width), jnp.float32),
        in_specs=[vmem] * 2,
        out_specs=vmem,
        compiler_params=pltpu.CompilerParams(vmem_limit_bytes=VMEM_LIMIT),
        cost_estimate=pl.CostEstimate(
            flops=2 * near.shape[0] * slots * LANES * width, bytes_accessed=4 * near.shape[0] * slots * width, transcendentals=0
        ),
        name="widen",
    )(near, spread)
    outputs = (
        jax.ShapeDtypeStruct((1, columns, nodes), jnp.bfloat16),
        jax.ShapeDtypeStruct((STEPS, columns), jnp.float32),
    )
    return pl.pallas_call(
        march_kernel,
        out_shape=outputs,
        in_specs=[vmem] * 5,
        out_specs=(hbm, hbm),
        scratch_shapes=[
            *(pltpu.VMEM(output.shape, output.dtype) for output in outputs),
            pltpu.SemaphoreType.DMA((2,)),
        ],
        compiler_params=pltpu.CompilerParams(vmem_limit_bytes=VMEM_LIMIT),
        name="march",
    )(near, far, wide, spread, rows)


def exchanged_plan(
    inverses, cotangent, subnet_sizes, slot_into, slot_from, offsets, weights, admittance, fault_bus
):
    block_count, column_count, node_count = cotangent.shape
    owner_count = lax.axis_size(OWNER_AXES)
    slot_depth = slot_into.shape[2]
    slot_count = owner_count * slot_depth
    local_span = block_count * node_count
    active = (jnp.arange(node_count, dtype=jnp.int32)[None, :] < subnet_sizes[:, None]).astype(
        jnp.float32
    )
    node_ids = jnp.arange(local_span, dtype=jnp.int32)[None, :]
    send_hot = (slot_into.reshape(slot_count)[:, None] == node_ids).astype(jnp.bfloat16)
    send_hot = send_hot.reshape(slot_count, block_count, node_count)
    from_local = slot_from.reshape(slot_count)
    is_used = (from_local >= 0).astype(jnp.float32)
    recv_hot = (
        (from_local[:, None] == node_ids)
        .astype(jnp.float32)
        .reshape(slot_count, block_count, node_count)
    )
    delay_steps = offsets.reshape(slot_count)
    fraction = weights.reshape(slot_count)
    conduct = admittance.reshape(slot_count) * is_used
    arrivals = {}
    results = {}
    for step_now in range(STEPS - 1, -1, -1):
        history = jnp.zeros((block_count, column_count, node_count), jnp.float32)
        terms = jnp.zeros((column_count, slot_count), jnp.float32)
        present = False
        for source_step in range(step_now + 2, min(step_now + 6, STEPS)):
            step_gap = source_step - step_now
            factor = conduct * (
                fraction * (delay_steps == step_gap).astype(jnp.float32)
                + (1.0 - fraction) * (delay_steps + 1 == step_gap).astype(jnp.float32)
            )
            terms = terms + factor[None, :] * arrivals[source_step].astype(jnp.float32)
            present = True
        if present:
            history = jnp.einsum("sk,kjn->jsn", terms, recv_hot, precision=lax.Precision.HIGHEST)
        if step_now == STEPS - 1:
            history = cotangent.astype(jnp.float32)
        driving = (history * active[:, None, :]).astype(jnp.bfloat16)
        adjoint = jnp.einsum("jsn,jnm->jsm", driving, inverses, preferred_element_type=jnp.float32)
        results[step_now] = (adjoint * active[:, None, :]).astype(jnp.bfloat16)
        if step_now >= 2:
            picked = jnp.einsum(
                "jsn,kjn->sk", results[step_now], send_hot, preferred_element_type=jnp.float32
            )
            arrivals[step_now] = lax.all_to_all(
                picked.astype(jnp.bfloat16)[None], OWNER_AXES, split_axis=2, concat_axis=2, tiled=True
            )[0]
    owner_index = lax.axis_index(OWNER_AXES)
    local_bus = fault_bus - owner_index * local_span
    owned = (local_bus >= 0) & (local_bus < local_span)
    clamped = jnp.clip(local_bus, 0, local_span - 1)
    position = (
        clamped // node_count * column_count * node_count
        + jnp.arange(column_count, dtype=jnp.int32) * node_count
        + clamped % node_count
    )
    sensitivity = jnp.stack(
        [
            jnp.where(
                owned, jnp.take(results[index].reshape(-1), position).astype(jnp.float32), 0.0
            )
            for index in range(STEPS)
        ]
    )
    return results[0], lax.psum(sensitivity, OWNER_AXES)


def per_device(*arrays):
    blocks, columns, nodes = arrays[1].shape
    owners, depth = arrays[3].shape[1:]
    slots = owners * depth
    fits = (
        blocks == 1
        and columns * 4 == LANES
        and depth == 8
        and lax.axis_size(OWNER_AXES[0]) == 4
        and lax.axis_size(OWNER_AXES[1]) == 2
        and slots + 2 * columns == LANES
        and nodes % LANES == 0
    )
    return gathered_plan(*arrays) if fits else exchanged_plan(*arrays)


def solution(mesh):
    return jax.shard_map(
        per_device,
        mesh=mesh,
        in_specs=(
            P(("groups", "sub", "half"), None, None),
            P(("groups", "sub", "half"), "scen", None),
            P(("groups", "sub", "half")),
            P(("groups", "sub", "half"), None, None),
            P(("groups", "sub", "half"), None, None),
            P(("groups", "sub", "half"), None, None),
            P(("groups", "sub", "half"), None, None),
            P(("groups", "sub", "half"), None, None),
            P(("groups", "scen")),
        ),
        out_specs=(P(("groups", "sub", "half"), "scen", None), P(None, ("groups", "scen"))),
        check_vma=False,
    )
```

```python
import jax
import jax.numpy as jnp
import numpy as np
from jax import lax
from jax.experimental import pallas as pl
from jax.experimental.pallas import tpu as pltpu
from jax.sharding import PartitionSpec as P

STEPS = 8
LANES = 128
VMEM_LIMIT = 16 * 2**20
HINT_FLOPS = 4 * 2**30
HINT_BYTES = 8 * 2**20
OWNER_AXES = ("sub", "half")
VARIANTS = (
    (2, 3, 0, 2),
    (2, 2, 3, 3),
    (4, 5, 0, 4),
    (2, 2, 0, 2),
    (0, 3, 0, 0),
    (4, 5, 3, 4),
)
NT = (((1,), (1,)), ((), ()))


def dot(left, right, dims=(((1,), (0,)), ((), ()))):
    return lax.dot_general(left, right, dims, preferred_element_type=jnp.float32)


def spread_matrix(column_count, owners):
    half = LANES // 2
    spread = np.zeros((LANES, (len(VARIANTS) + 2) * LANES), np.float32)
    for variant, gaps in enumerate(VARIANTS):
        for quarter, gap in enumerate(gaps):
            lane = variant * LANES + quarter * column_count
            for piece in range(3 * (gap - 2), 3 * (gap - 1)) if gap else ():
                for owner in range(owners):
                    spread[piece // 8 * half + owner * 8 + piece % 8, lane : lane + column_count] = 1
    for lane in range(LANES):
        for part in range(2):
            start = half + part * column_count
            spread[start + lane % column_count, (len(VARIANTS) + part) * LANES + lane] = 1
    return spread


SOURCES = ((1, 0, 3, 2), (2, 3, 1, 0), (3, 2, 0, 1))
HELD = (0, 3, 5, 7, 1, 2, 4, 6)


def column_of(ref, place):
    _, peers, depth = ref.shape
    eye = lax.broadcasted_iota(jnp.int32, (depth, depth), 0) == lax.broadcasted_iota(
        jnp.int32, (depth, depth), 1
    )
    rows = [
        jnp.where(eye, jnp.broadcast_to(row.astype(jnp.float32), (depth, depth)), 0.0)
        for row in (ref[0, pl.ds(lax.bitwise_xor(place, jnp.int32(apart)), 1), :] for apart in range(peers))
    ]
    return jnp.sum(jnp.concatenate(rows, axis=0), axis=1, keepdims=True)


def owner_here():
    return lax.axis_index(OWNER_AXES[0]) * lax.axis_size(OWNER_AXES[1]) + lax.axis_index(OWNER_AXES[1])


def lane_kernel(lane_ref):
    lane_ref[...] = lax.broadcasted_iota(jnp.int32, lane_ref.shape, 1).astype(jnp.float32)


def pick_kernel(
    packed_ref, lane_ref, into_ref, from_ref, offset_ref, weight_ref, admit_ref, inverse_ref, cotangent_ref,
    message_ref, rows_ref,
):
    nodes = inverse_ref.shape[1]
    _, peers, depth = into_ref.shape
    slots = peers * depth
    columns = cotangent_ref.shape[1]
    lane_f = jnp.broadcast_to(lane_ref[:1], (slots, nodes))
    live = packed_ref[:, :1]
    alive = lane_f < live.astype(jnp.float32)
    place = owner_here()
    into = column_of(into_ref, place)
    source = column_of(from_ref, place)
    recv_hot = jnp.where((source == lane_f) & alive, 1.0, 0.0).astype(jnp.bfloat16)
    send_hot = jnp.where(into == lane_f, 1.0, 0.0).astype(jnp.bfloat16)
    driving = jnp.where(alive[:columns], cotangent_ref[0].astype(jnp.float32), 0.0).astype(jnp.bfloat16)
    stack = jnp.concatenate([recv_hot, driving], axis=0)
    picked = dot(stack, inverse_ref[0])
    lane = lax.broadcasted_iota(jnp.int32, picked.shape, 1)
    picked = jnp.where(lane < live, picked, 0.0).astype(jnp.bfloat16)
    width = columns + 1
    bus = (packed_ref[...] - place * nodes).astype(jnp.float32)
    eye = lax.broadcasted_iota(jnp.int32, (columns, width), 0) + 1 == lax.broadcasted_iota(
        jnp.int32, (columns, width), 1
    )
    bus = jnp.sum(jnp.where(eye, jnp.broadcast_to(bus, (columns, width)), 0.0), axis=1, keepdims=True)
    fault_hot = jnp.where(bus == lane_f[:columns], 1.0, 0.0).astype(jnp.bfloat16)
    delay = column_of(offset_ref, place)
    weight = column_of(weight_ref, place)
    admit = column_of(admit_ref, place)
    conduct = jnp.where(source >= 0, admit, 0.0)
    near, far = conduct * weight, conduct * (1.0 - weight)
    factors = [
        jnp.where(delay == 2, near, 0.0),
        jnp.where(delay == 3, near, 0.0) + jnp.where(delay == 2, far, 0.0),
        jnp.where(delay == 4, near, 0.0) + jnp.where(delay == 3, far, 0.0),
        jnp.where(delay == 4, far, 0.0),
    ]
    pieces = []
    for factor in factors:
        for _ in range(3):
            part = factor.astype(jnp.bfloat16).astype(jnp.float32)
            factor = factor - part
            pieces.append(part)
    spot = lax.broadcasted_iota(jnp.int32, (slots, LANES), 1)
    upper = jnp.zeros((slots, LANES), jnp.float32)
    lower = jnp.zeros((slots, LANES), jnp.float32)
    for index, piece in enumerate(pieces):
        if index < 8:
            upper = jnp.where(spot == index, piece, upper)
        else:
            lower = jnp.where(spot == index - 8, piece, lower)
    eye = jnp.where(
        lax.broadcasted_iota(jnp.int32, (8, LANES), 0) == lax.broadcasted_iota(jnp.int32, (8, LANES), 1), 1.0, 0.0
    ).astype(jnp.bfloat16)
    table = dot(eye, jnp.concatenate([upper, lower], axis=0).astype(jnp.bfloat16), NT)
    rows = picked[:slots]
    rows_ref[...] = rows
    blank = jnp.zeros((columns, nodes), jnp.bfloat16)
    body = dot(send_hot, jnp.concatenate([picked, blank], axis=0), NT) + dot(
        rows, jnp.concatenate([blank] * (slots // columns + 1) + [fault_hot], axis=0), NT
    )
    found = jnp.concatenate([blank] * (slots // columns) + [picked[slots:] * fault_hot, blank], axis=0)
    last = jnp.where(lax.broadcasted_iota(jnp.int32, (8, nodes), 0) == 7, 1.0, 0.0).astype(jnp.bfloat16)
    table = table + dot(last, found, NT)
    message_ref[...] = jnp.concatenate([body, table], axis=0).astype(jnp.bfloat16)


def lanes(value, index):
    return value[:, LANES * index : LANES * (index + 1)]


def turned_pieces(messages):
    slots = LANES // 2
    tables = [message[slots:].astype(jnp.float32) for message in messages]
    filled = tables + [jnp.zeros((8, LANES), jnp.float32)] * (8 - len(tables))
    turned = jnp.concatenate(filled * 2, axis=0).T
    lane = lax.broadcasted_iota(jnp.int32, (slots, LANES), 1)
    turned = jnp.where(lane < LANES // 2, turned[:slots], turned[slots:])
    group = lane % (LANES // 2) // 8
    return [jnp.where(group == index, turned, 0.0).astype(jnp.bfloat16) for index in range(len(messages))]


def widen_kernel(near_ref, spread_ref, wide_ref):
    messages = [near_ref[p] for p in range(near_ref.shape[0])]
    count = LANES * len(VARIANTS)
    for index, piece in enumerate(turned_pieces(messages)):
        wide_ref[index, :, :count] = dot(piece, spread_ref[:, :count])
        wide_ref[index, :, count:] = dot(messages[index][: LANES // 2], spread_ref[:, count:])


def march_kernel(
    near_ref, far_ref, wide_ref, spread_ref, rows_ref, first_hbm, fault_hbm, first_ref, fault_ref, semaphores
):
    held = (near_ref, far_ref)
    owners = sum(ref.shape[0] for ref in held)
    slots = rows_ref.shape[0]
    columns = first_ref.shape[1]
    depth = slots // owners
    count = len(VARIANTS)
    order = HELD
    spot = {apart: index for index, apart in enumerate(order)}

    def exchange(parts):
        return [
            jnp.concatenate(
                [parts[spot[mine ^ other]][depth * other : depth * (other + 1)] for other in range(owners)], axis=0
            )
            for mine in order
        ]

    def rounded(value):
        return value.astype(jnp.bfloat16).astype(jnp.float32)

    blocks = [ref[p] for ref in held for p in range(ref.shape[0])]
    system = [block[:slots, :slots] for block in blocks]
    fresh = blocks[-far_ref.shape[0] :]
    pieces = turned_pieces(fresh)

    def spread_of(index, sources):
        pair = slice(LANES * index, LANES * (index + 2))
        known = [wide_ref[p, :, pair] for p in range(wide_ref.shape[0])]
        both = known + [dot(source, spread_ref[:, pair]) for source in sources]
        return [lanes(part, 0) for part in both], [lanes(part, 1) for part in both]

    seven, fault = spread_of(count, [block[:slots] for block in fresh])
    seven = exchange(seven)
    factor = [*spread_of(0, pieces)]

    def seen(drive):
        total = fault[0] * drive[0].astype(jnp.float32)
        for o in range(1, owners):
            total = total + fault[o] * drive[o].astype(jnp.float32)
        return rounded(jnp.sum(total, axis=0, keepdims=True))

    near = [(factor[0][o] * seven[o]).astype(jnp.bfloat16) for o in range(owners)]
    wide = [(factor[1][o] * seven[o]).astype(jnp.bfloat16) for o in range(owners)]
    result = [dot(system[o], jnp.concatenate([near[o], wide[o]], axis=1)) for o in range(owners)]
    factor += [*spread_of(2, pieces), *spread_of(4, pieces)]
    row_a = seen(near)
    arrived = exchange([rounded(part) for part in result])
    drive = [
        factor[2][o] * seven[o] + factor[3][o] * lanes(arrived[o], 0) + factor[4][o] * lanes(arrived[o], 1)
        for o in range(owners)
    ]
    drive = [part.astype(jnp.bfloat16) for part in drive]
    later = [factor[5][o] * lanes(arrived[o], 1) for o in range(owners)]
    result = [dot(system[o], drive[o]) for o in range(owners)]
    row_b = seen(drive)
    arrived = exchange([rounded(part) for part in result])
    later = [later[o] + factor[1][o] * arrived[o] for o in range(owners)]
    drive = [part + pltpu.roll(part, 2 * columns, 1) for part in later]
    own = drive[0].T[columns : 2 * columns].astype(jnp.bfloat16)
    first_ref[0] = dot(own, rows_ref[...]).astype(jnp.bfloat16)
    save_first = pltpu.make_async_copy(first_ref, first_hbm, semaphores.at[0])
    save_first.start()
    row_c = seen([part.astype(jnp.bfloat16) for part in drive])
    row_s = sum(block[slots + 7 : slots + 8].astype(jnp.float32) for block in blocks)

    def back(value, quarters):
        return pltpu.roll(value, LANES - quarters * columns, 1)

    table = [
        back(row_c, 1),
        row_c,
        back(row_b, 1),
        row_b,
        back(row_a, 1),
        row_a,
        jnp.zeros_like(row_a),
        back(row_s, 2),
    ]
    step = lax.broadcasted_iota(jnp.int32, (STEPS, LANES), 0)
    total = jnp.zeros((STEPS, LANES), jnp.float32)
    for index, value in enumerate(table):
        total = jnp.where(step == index, jnp.broadcast_to(value, total.shape), total)
    fault_ref[...] = total[:, :columns]
    save_fault = pltpu.make_async_copy(fault_ref, fault_hbm, semaphores.at[1])
    save_fault.start()
    save_first.wait()
    save_fault.wait()


def gathered_plan(
    inverses, cotangent, subnet_sizes, slot_into, slot_from, offsets, weights, admittance, fault_bus
):
    _, columns, nodes = cotangent.shape
    owners, depth = slot_into.shape[1:]
    slots = owners * depth
    height = slots + 8
    vmem = pl.BlockSpec(memory_space=pltpu.VMEM)
    hbm = pl.BlockSpec(memory_space=pltpu.HBM)
    lane = pl.pallas_call(
        lane_kernel,
        out_shape=jax.ShapeDtypeStruct((8, nodes), jnp.float32),
        out_specs=vmem,
        compiler_params=pltpu.CompilerParams(vmem_limit_bytes=VMEM_LIMIT),
        cost_estimate=pl.CostEstimate(flops=HINT_FLOPS, bytes_accessed=HINT_BYTES, transcendentals=0),
        name="lane",
    )()
    packed = jnp.concatenate([subnet_sizes, fault_bus])[None]
    arrays = (packed, lane, slot_into, slot_from, offsets, weights, admittance, inverses, cotangent)
    message, rows = pl.pallas_call(
        pick_kernel,
        out_shape=(
            jax.ShapeDtypeStruct((height, LANES), jnp.bfloat16),
            jax.ShapeDtypeStruct((slots, nodes), jnp.bfloat16),
        ),
        in_specs=[vmem] * len(arrays),
        out_specs=(vmem, vmem),
        compiler_params=pltpu.CompilerParams(vmem_limit_bytes=VMEM_LIMIT),
        name="pick",
    )(*arrays)
    spread = jnp.asarray(spread_matrix(columns, 8), jnp.bfloat16)
    width = spread.shape[1]


    def send(held, sources):
        pairs = [(2 * source + core, 2 * z + 1 - core) for z, source in enumerate(sources) for core in range(2)]
        return lax.ppermute(held, OWNER_AXES, pairs)

    own = message[None]
    beside, second, third = (send(own, sources) for sources in SOURCES)
    low = lax.axis_index(OWNER_AXES[0]) < 2
    near = jnp.concatenate([own, beside, jnp.where(low, second, third), jnp.where(low, third, second)], axis=0)
    far = send(near, range(len(SOURCES) + 1))
    wide = pl.pallas_call(
        widen_kernel,
        out_shape=jax.ShapeDtypeStruct((near.shape[0], slots, width), jnp.float32),
        in_specs=[vmem] * 2,
        out_specs=vmem,
        compiler_params=pltpu.CompilerParams(vmem_limit_bytes=VMEM_LIMIT),
        cost_estimate=pl.CostEstimate(
            flops=2 * near.shape[0] * slots * LANES * width, bytes_accessed=4 * near.shape[0] * slots * width, transcendentals=0
        ),
        name="widen",
    )(near, spread)
    outputs = (
        jax.ShapeDtypeStruct((1, columns, nodes), jnp.bfloat16),
        jax.ShapeDtypeStruct((STEPS, columns), jnp.float32),
    )
    return pl.pallas_call(
        march_kernel,
        out_shape=outputs,
        in_specs=[vmem] * 5,
        out_specs=(hbm, hbm),
        scratch_shapes=[
            *(pltpu.VMEM(output.shape, output.dtype) for output in outputs),
            pltpu.SemaphoreType.DMA((2,)),
        ],
        compiler_params=pltpu.CompilerParams(vmem_limit_bytes=VMEM_LIMIT),
        name="march",
    )(near, far, wide, spread, rows)


def exchanged_plan(
    inverses, cotangent, subnet_sizes, slot_into, slot_from, offsets, weights, admittance, fault_bus
):
    block_count, column_count, node_count = cotangent.shape
    owner_count = lax.axis_size(OWNER_AXES)
    slot_depth = slot_into.shape[2]
    slot_count = owner_count * slot_depth
    local_span = block_count * node_count
    active = (jnp.arange(node_count, dtype=jnp.int32)[None, :] < subnet_sizes[:, None]).astype(
        jnp.float32
    )
    node_ids = jnp.arange(local_span, dtype=jnp.int32)[None, :]
    send_hot = (slot_into.reshape(slot_count)[:, None] == node_ids).astype(jnp.bfloat16)
    send_hot = send_hot.reshape(slot_count, block_count, node_count)
    from_local = slot_from.reshape(slot_count)
    is_used = (from_local >= 0).astype(jnp.float32)
    recv_hot = (
        (from_local[:, None] == node_ids)
        .astype(jnp.float32)
        .reshape(slot_count, block_count, node_count)
    )
    delay_steps = offsets.reshape(slot_count)
    fraction = weights.reshape(slot_count)
    conduct = admittance.reshape(slot_count) * is_used
    arrivals = {}
    results = {}
    for step_now in range(STEPS - 1, -1, -1):
        history = jnp.zeros((block_count, column_count, node_count), jnp.float32)
        terms = jnp.zeros((column_count, slot_count), jnp.float32)
        present = False
        for source_step in range(step_now + 2, min(step_now + 6, STEPS)):
            step_gap = source_step - step_now
            factor = conduct * (
                fraction * (delay_steps == step_gap).astype(jnp.float32)
                + (1.0 - fraction) * (delay_steps + 1 == step_gap).astype(jnp.float32)
            )
            terms = terms + factor[None, :] * arrivals[source_step].astype(jnp.float32)
            present = True
        if present:
            history = jnp.einsum("sk,kjn->jsn", terms, recv_hot, precision=lax.Precision.HIGHEST)
        if step_now == STEPS - 1:
            history = cotangent.astype(jnp.float32)
        driving = (history * active[:, None, :]).astype(jnp.bfloat16)
        adjoint = jnp.einsum("jsn,jnm->jsm", driving, inverses, preferred_element_type=jnp.float32)
        results[step_now] = (adjoint * active[:, None, :]).astype(jnp.bfloat16)
        if step_now >= 2:
            picked = jnp.einsum(
                "jsn,kjn->sk", results[step_now], send_hot, preferred_element_type=jnp.float32
            )
            arrivals[step_now] = lax.all_to_all(
                picked.astype(jnp.bfloat16)[None], OWNER_AXES, split_axis=2, concat_axis=2, tiled=True
            )[0]
    owner_index = lax.axis_index(OWNER_AXES)
    local_bus = fault_bus - owner_index * local_span
    owned = (local_bus >= 0) & (local_bus < local_span)
    clamped = jnp.clip(local_bus, 0, local_span - 1)
    position = (
        clamped // node_count * column_count * node_count
        + jnp.arange(column_count, dtype=jnp.int32) * node_count
        + clamped % node_count
    )
    sensitivity = jnp.stack(
        [
            jnp.where(
                owned, jnp.take(results[index].reshape(-1), position).astype(jnp.float32), 0.0
            )
            for index in range(STEPS)
        ]
    )
    return results[0], lax.psum(sensitivity, OWNER_AXES)


def per_device(*arrays):
    blocks, columns, nodes = arrays[1].shape
    owners, depth = arrays[3].shape[1:]
    slots = owners * depth
    fits = (
        blocks == 1
        and columns * 4 == LANES
        and depth == 8
        and lax.axis_size(OWNER_AXES[0]) == 4
        and lax.axis_size(OWNER_AXES[1]) == 2
        and slots + 2 * columns == LANES
        and nodes % LANES == 0
    )
    return gathered_plan(*arrays) if fits else exchanged_plan(*arrays)


def solution(mesh):
    return jax.shard_map(
        per_device,
        mesh=mesh,
        in_specs=(
            P(("groups", "sub", "half"), None, None),
            P(("groups", "sub", "half"), "scen", None),
            P(("groups", "sub", "half")),
            P(("groups", "sub", "half"), None, None),
            P(("groups", "sub", "half"), None, None),
            P(("groups", "sub", "half"), None, None),
            P(("groups", "sub", "half"), None, None),
            P(("groups", "sub", "half"), None, None),
            P(("groups", "scen")),
        ),
        out_specs=(P(("groups", "sub", "half"), "scen", None), P(None, ("groups", "scen"))),
        check_vma=False,
    )
```

```python
import jax
import jax.numpy as jnp
import numpy as np
from jax import lax
from jax.experimental import pallas as pl
from jax.experimental.pallas import tpu as pltpu
from jax.sharding import PartitionSpec as P

STEPS = 8
LANES = 128
VMEM_LIMIT = 16 * 2**20
HINT_FLOPS = 4 * 2**30
HINT_BYTES = 8 * 2**20
OWNER_AXES = ("sub", "half")
VARIANTS = (
    (2, 3, 0, 2),
    (2, 2, 3, 3),
    (4, 5, 0, 4),
    (2, 2, 0, 2),
    (0, 3, 0, 0),
    (4, 5, 3, 4),
)
NT = (((1,), (1,)), ((), ()))


def dot(left, right, dims=(((1,), (0,)), ((), ()))):
    return lax.dot_general(left, right, dims, preferred_element_type=jnp.float32)


def spread_matrix(column_count, owners):
    half = LANES // 2
    spread = np.zeros((LANES, (len(VARIANTS) + 2) * LANES), np.float32)
    for variant, gaps in enumerate(VARIANTS):
        for quarter, gap in enumerate(gaps):
            lane = variant * LANES + quarter * column_count
            for piece in range(3 * (gap - 2), 3 * (gap - 1)) if gap else ():
                for owner in range(owners):
                    spread[piece // 8 * half + owner * 8 + piece % 8, lane : lane + column_count] = 1
    for lane in range(LANES):
        for part in range(2):
            start = half + part * column_count
            spread[start + lane % column_count, (len(VARIANTS) + part) * LANES + lane] = 1
    return spread


SOURCES = ((1, 0, 3, 2), (2, 3, 1, 0), (3, 2, 0, 1))
HELD = (0, 3, 5, 7, 1, 2, 4, 6)


def column_of(ref, place):
    _, peers, depth = ref.shape
    eye = lax.broadcasted_iota(jnp.int32, (depth, depth), 0) == lax.broadcasted_iota(
        jnp.int32, (depth, depth), 1
    )
    rows = [
        jnp.where(eye, jnp.broadcast_to(row.astype(jnp.float32), (depth, depth)), 0.0)
        for row in (ref[0, pl.ds(lax.bitwise_xor(place, jnp.int32(apart)), 1), :] for apart in range(peers))
    ]
    return jnp.sum(jnp.concatenate(rows, axis=0), axis=1, keepdims=True)


def owner_here():
    return lax.axis_index(OWNER_AXES[0]) * lax.axis_size(OWNER_AXES[1]) + lax.axis_index(OWNER_AXES[1])


def lane_kernel(lane_ref):
    lane_ref[...] = lax.broadcasted_iota(jnp.int32, lane_ref.shape, 1).astype(jnp.float32)


def pick_kernel(
    packed_ref, lane_ref, into_ref, from_ref, offset_ref, weight_ref, admit_ref, inverse_ref, cotangent_ref,
    message_ref, rows_ref,
):
    nodes = inverse_ref.shape[1]
    _, peers, depth = into_ref.shape
    slots = peers * depth
    columns = cotangent_ref.shape[1]
    lane_f = jnp.broadcast_to(lane_ref[:1], (slots, nodes))
    live = packed_ref[:, :1]
    alive = lane_f < live.astype(jnp.float32)
    place = owner_here()
    into = column_of(into_ref, place)
    source = column_of(from_ref, place)
    recv_hot = jnp.where((source == lane_f) & alive, 1.0, 0.0).astype(jnp.bfloat16)
    send_hot = jnp.where(into == lane_f, 1.0, 0.0).astype(jnp.bfloat16)
    driving = jnp.where(alive[:columns], cotangent_ref[0].astype(jnp.float32), 0.0).astype(jnp.bfloat16)
    stack = jnp.concatenate([recv_hot, driving], axis=0)
    picked = dot(stack, inverse_ref[0])
    lane = lax.broadcasted_iota(jnp.int32, picked.shape, 1)
    picked = jnp.where(lane < live, picked, 0.0).astype(jnp.bfloat16)
    width = columns + 1
    bus = (packed_ref[...] - place * nodes).astype(jnp.float32)
    eye = lax.broadcasted_iota(jnp.int32, (columns, width), 0) + 1 == lax.broadcasted_iota(
        jnp.int32, (columns, width), 1
    )
    bus = jnp.sum(jnp.where(eye, jnp.broadcast_to(bus, (columns, width)), 0.0), axis=1, keepdims=True)
    fault_hot = jnp.where(bus == lane_f[:columns], 1.0, 0.0).astype(jnp.bfloat16)
    delay = column_of(offset_ref, place)
    weight = column_of(weight_ref, place)
    admit = column_of(admit_ref, place)
    conduct = jnp.where(source >= 0, admit, 0.0)
    near, far = conduct * weight, conduct * (1.0 - weight)
    factors = [
        jnp.where(delay == 2, near, 0.0),
        jnp.where(delay == 3, near, 0.0) + jnp.where(delay == 2, far, 0.0),
        jnp.where(delay == 4, near, 0.0) + jnp.where(delay == 3, far, 0.0),
        jnp.where(delay == 4, far, 0.0),
    ]
    pieces = []
    for factor in factors:
        for _ in range(3):
            part = factor.astype(jnp.bfloat16).astype(jnp.float32)
            factor = factor - part
            pieces.append(part)
    spot = lax.broadcasted_iota(jnp.int32, (slots, LANES), 1)
    upper = jnp.zeros((slots, LANES), jnp.float32)
    lower = jnp.zeros((slots, LANES), jnp.float32)
    for index, piece in enumerate(pieces):
        if index < 8:
            upper = jnp.where(spot == index, piece, upper)
        else:
            lower = jnp.where(spot == index - 8, piece, lower)
    eye = jnp.where(
        lax.broadcasted_iota(jnp.int32, (8, LANES), 0) == lax.broadcasted_iota(jnp.int32, (8, LANES), 1), 1.0, 0.0
    ).astype(jnp.bfloat16)
    table = dot(eye, jnp.concatenate([upper, lower], axis=0).astype(jnp.bfloat16), NT)
    rows = picked[:slots]
    rows_ref[...] = rows
    blank = jnp.zeros((columns, nodes), jnp.bfloat16)
    body = dot(send_hot, jnp.concatenate([picked, blank], axis=0), NT) + dot(
        rows, jnp.concatenate([blank] * (slots // columns + 1) + [fault_hot], axis=0), NT
    )
    found = jnp.concatenate([blank] * (slots // columns) + [picked[slots:] * fault_hot, blank], axis=0)
    last = jnp.where(lax.broadcasted_iota(jnp.int32, (8, nodes), 0) == 7, 1.0, 0.0).astype(jnp.bfloat16)
    table = table + dot(last, found, NT)
    message_ref[...] = jnp.concatenate([body, table], axis=0).astype(jnp.bfloat16)


def lanes(value, index):
    return value[:, LANES * index : LANES * (index + 1)]


def turned_pieces(messages):
    slots = LANES // 2
    tables = [message[slots:].astype(jnp.float32) for message in messages]
    filled = tables + [jnp.zeros((8, LANES), jnp.float32)] * (8 - len(tables))
    turned = jnp.concatenate(filled * 2, axis=0).T
    lane = lax.broadcasted_iota(jnp.int32, (slots, LANES), 1)
    turned = jnp.where(lane < LANES // 2, turned[:slots], turned[slots:])
    group = lane % (LANES // 2) // 8
    return [jnp.where(group == index, turned, 0.0).astype(jnp.bfloat16) for index in range(len(messages))]


def widen_kernel(near_ref, spread_ref, wide_ref):
    messages = [near_ref[p] for p in range(near_ref.shape[0])]
    count = LANES * len(VARIANTS)
    for index, piece in enumerate(turned_pieces(messages)):
        wide_ref[index, :, :count] = dot(piece, spread_ref[:, :count])
        wide_ref[index, :, count:] = dot(messages[index][: LANES // 2], spread_ref[:, count:])


def march_kernel(
    near_ref, far_ref, wide_ref, spread_ref, rows_ref, first_hbm, fault_hbm, first_ref, fault_ref, semaphores
):
    held = (near_ref, far_ref)
    owners = sum(ref.shape[0] for ref in held)
    slots = rows_ref.shape[0]
    columns = first_ref.shape[1]
    depth = slots // owners
    count = len(VARIANTS)
    order = HELD
    spot = {apart: index for index, apart in enumerate(order)}

    def exchange(parts):
        return [
            jnp.concatenate(
                [parts[spot[mine ^ other]][depth * other : depth * (other + 1)] for other in range(owners)], axis=0
            )
            for mine in order
        ]

    def rounded(value):
        return value.astype(jnp.bfloat16).astype(jnp.float32)

    blocks = [ref[p] for ref in held for p in range(ref.shape[0])]
    system = [block[:slots, :slots] for block in blocks]
    fresh = blocks[-far_ref.shape[0] :]
    pieces = turned_pieces(fresh)

    def spread_of(index, sources):
        pair = slice(LANES * index, LANES * (index + 2))
        known = [wide_ref[p, :, pair] for p in range(wide_ref.shape[0])]
        both = known + [dot(source, spread_ref[:, pair]) for source in sources]
        return [lanes(part, 0) for part in both], [lanes(part, 1) for part in both]

    seven, fault = spread_of(count, [block[:slots] for block in fresh])
    factor = [*spread_of(0, pieces)]
    seven = exchange(seven)

    def seen(drive):
        total = fault[0] * drive[0].astype(jnp.float32)
        for o in range(1, owners):
            total = total + fault[o] * drive[o].astype(jnp.float32)
        return rounded(jnp.sum(total, axis=0, keepdims=True))

    near = [(factor[0][o] * seven[o]).astype(jnp.bfloat16) for o in range(owners)]
    wide = [(factor[1][o] * seven[o]).astype(jnp.bfloat16) for o in range(owners)]
    result = [dot(system[o], jnp.concatenate([near[o], wide[o]], axis=1)) for o in range(owners)]
    factor += [*spread_of(2, pieces), *spread_of(4, pieces)]
    row_a = seen(near)
    arrived = exchange([rounded(part) for part in result])
    drive = [
        factor[2][o] * seven[o] + factor[3][o] * lanes(arrived[o], 0) + factor[4][o] * lanes(arrived[o], 1)
        for o in range(owners)
    ]
    drive = [part.astype(jnp.bfloat16) for part in drive]
    later = [factor[5][o] * lanes(arrived[o], 1) for o in range(owners)]
    result = [dot(system[o], drive[o]) for o in range(owners)]
    row_b = seen(drive)
    arrived = exchange([rounded(part) for part in result])
    later = [later[o] + factor[1][o] * arrived[o] for o in range(owners)]
    turned = later[0].T
    own = (turned[columns : 2 * columns] + turned[3 * columns :]).astype(jnp.bfloat16)
    first_ref[0] = dot(own, rows_ref[...]).astype(jnp.bfloat16)
    save_first = pltpu.make_async_copy(first_ref, first_hbm, semaphores.at[0])
    save_first.start()
    row_c = seen([(part + pltpu.roll(part, 2 * columns, 1)).astype(jnp.bfloat16) for part in later])
    row_s = sum(block[slots + 7 : slots + 8].astype(jnp.float32) for block in blocks)

    def back(value, quarters):
        return pltpu.roll(value, LANES - quarters * columns, 1)

    table = [
        back(row_c, 1),
        row_c,
        back(row_b, 1),
        row_b,
        back(row_a, 1),
        row_a,
        jnp.zeros_like(row_a),
        back(row_s, 2),
    ]
    step = lax.broadcasted_iota(jnp.int32, (STEPS, LANES), 0)
    total = jnp.zeros((STEPS, LANES), jnp.float32)
    for index, value in enumerate(table):
        total = jnp.where(step == index, jnp.broadcast_to(value, total.shape), total)
    fault_ref[...] = total[:, :columns]
    save_fault = pltpu.make_async_copy(fault_ref, fault_hbm, semaphores.at[1])
    save_fault.start()
    save_first.wait()
    save_fault.wait()


def gathered_plan(
    inverses, cotangent, subnet_sizes, slot_into, slot_from, offsets, weights, admittance, fault_bus
):
    _, columns, nodes = cotangent.shape
    owners, depth = slot_into.shape[1:]
    slots = owners * depth
    height = slots + 8
    vmem = pl.BlockSpec(memory_space=pltpu.VMEM)
    hbm = pl.BlockSpec(memory_space=pltpu.HBM)
    lane = pl.pallas_call(
        lane_kernel,
        out_shape=jax.ShapeDtypeStruct((8, nodes), jnp.float32),
        out_specs=vmem,
        compiler_params=pltpu.CompilerParams(vmem_limit_bytes=VMEM_LIMIT),
        cost_estimate=pl.CostEstimate(flops=HINT_FLOPS, bytes_accessed=HINT_BYTES, transcendentals=0),
        name="lane",
    )()
    packed = jnp.concatenate([subnet_sizes, fault_bus])[None]
    arrays = (packed, lane, slot_into, slot_from, offsets, weights, admittance, inverses, cotangent)
    message, rows = pl.pallas_call(
        pick_kernel,
        out_shape=(
            jax.ShapeDtypeStruct((height, LANES), jnp.bfloat16),
            jax.ShapeDtypeStruct((slots, nodes), jnp.bfloat16),
        ),
        in_specs=[vmem] * len(arrays),
        out_specs=(vmem, vmem),
        compiler_params=pltpu.CompilerParams(vmem_limit_bytes=VMEM_LIMIT),
        name="pick",
    )(*arrays)
    spread = jnp.asarray(spread_matrix(columns, 8), jnp.bfloat16)
    width = spread.shape[1]


    def send(held, sources):
        pairs = [(2 * source + core, 2 * z + 1 - core) for z, source in enumerate(sources) for core in range(2)]
        return lax.ppermute(held, OWNER_AXES, pairs)

    own = message[None]
    beside, second, third = (send(own, sources) for sources in SOURCES)
    low = lax.axis_index(OWNER_AXES[0]) < 2
    near = jnp.concatenate([own, beside, jnp.where(low, second, third), jnp.where(low, third, second)], axis=0)
    far = send(near, range(len(SOURCES) + 1))
    wide = pl.pallas_call(
        widen_kernel,
        out_shape=jax.ShapeDtypeStruct((near.shape[0], slots, width), jnp.float32),
        in_specs=[vmem] * 2,
        out_specs=vmem,
        compiler_params=pltpu.CompilerParams(vmem_limit_bytes=VMEM_LIMIT),
        cost_estimate=pl.CostEstimate(
            flops=2 * near.shape[0] * slots * LANES * width, bytes_accessed=4 * near.shape[0] * slots * width, transcendentals=0
        ),
        name="widen",
    )(near, spread)
    outputs = (
        jax.ShapeDtypeStruct((1, columns, nodes), jnp.bfloat16),
        jax.ShapeDtypeStruct((STEPS, columns), jnp.float32),
    )
    return pl.pallas_call(
        march_kernel,
        out_shape=outputs,
        in_specs=[vmem] * 5,
        out_specs=(hbm, hbm),
        scratch_shapes=[
            *(pltpu.VMEM(output.shape, output.dtype) for output in outputs),
            pltpu.SemaphoreType.DMA((2,)),
        ],
        compiler_params=pltpu.CompilerParams(vmem_limit_bytes=VMEM_LIMIT),
        name="march",
    )(near, far, wide, spread, rows)


def exchanged_plan(
    inverses, cotangent, subnet_sizes, slot_into, slot_from, offsets, weights, admittance, fault_bus
):
    block_count, column_count, node_count = cotangent.shape
    owner_count = lax.axis_size(OWNER_AXES)
    slot_depth = slot_into.shape[2]
    slot_count = owner_count * slot_depth
    local_span = block_count * node_count
    active = (jnp.arange(node_count, dtype=jnp.int32)[None, :] < subnet_sizes[:, None]).astype(
        jnp.float32
    )
    node_ids = jnp.arange(local_span, dtype=jnp.int32)[None, :]
    send_hot = (slot_into.reshape(slot_count)[:, None] == node_ids).astype(jnp.bfloat16)
    send_hot = send_hot.reshape(slot_count, block_count, node_count)
    from_local = slot_from.reshape(slot_count)
    is_used = (from_local >= 0).astype(jnp.float32)
    recv_hot = (
        (from_local[:, None] == node_ids)
        .astype(jnp.float32)
        .reshape(slot_count, block_count, node_count)
    )
    delay_steps = offsets.reshape(slot_count)
    fraction = weights.reshape(slot_count)
    conduct = admittance.reshape(slot_count) * is_used
    arrivals = {}
    results = {}
    for step_now in range(STEPS - 1, -1, -1):
        history = jnp.zeros((block_count, column_count, node_count), jnp.float32)
        terms = jnp.zeros((column_count, slot_count), jnp.float32)
        present = False
        for source_step in range(step_now + 2, min(step_now + 6, STEPS)):
            step_gap = source_step - step_now
            factor = conduct * (
                fraction * (delay_steps == step_gap).astype(jnp.float32)
                + (1.0 - fraction) * (delay_steps + 1 == step_gap).astype(jnp.float32)
            )
            terms = terms + factor[None, :] * arrivals[source_step].astype(jnp.float32)
            present = True
        if present:
            history = jnp.einsum("sk,kjn->jsn", terms, recv_hot, precision=lax.Precision.HIGHEST)
        if step_now == STEPS - 1:
            history = cotangent.astype(jnp.float32)
        driving = (history * active[:, None, :]).astype(jnp.bfloat16)
        adjoint = jnp.einsum("jsn,jnm->jsm", driving, inverses, preferred_element_type=jnp.float32)
        results[step_now] = (adjoint * active[:, None, :]).astype(jnp.bfloat16)
        if step_now >= 2:
            picked = jnp.einsum(
                "jsn,kjn->sk", results[step_now], send_hot, preferred_element_type=jnp.float32
            )
            arrivals[step_now] = lax.all_to_all(
                picked.astype(jnp.bfloat16)[None], OWNER_AXES, split_axis=2, concat_axis=2, tiled=True
            )[0]
    owner_index = lax.axis_index(OWNER_AXES)
    local_bus = fault_bus - owner_index * local_span
    owned = (local_bus >= 0) & (local_bus < local_span)
    clamped = jnp.clip(local_bus, 0, local_span - 1)
    position = (
        clamped // node_count * column_count * node_count
        + jnp.arange(column_count, dtype=jnp.int32) * node_count
        + clamped % node_count
    )
    sensitivity = jnp.stack(
        [
            jnp.where(
                owned, jnp.take(results[index].reshape(-1), position).astype(jnp.float32), 0.0
            )
            for index in range(STEPS)
        ]
    )
    return results[0], lax.psum(sensitivity, OWNER_AXES)


def per_device(*arrays):
    blocks, columns, nodes = arrays[1].shape
    owners, depth = arrays[3].shape[1:]
    slots = owners * depth
    fits = (
        blocks == 1
        and columns * 4 == LANES
        and depth == 8
        and lax.axis_size(OWNER_AXES[0]) == 4
        and lax.axis_size(OWNER_AXES[1]) == 2
        and slots + 2 * columns == LANES
        and nodes % LANES == 0
    )
    return gathered_plan(*arrays) if fits else exchanged_plan(*arrays)


def solution(mesh):
    return jax.shard_map(
        per_device,
        mesh=mesh,
        in_specs=(
            P(("groups", "sub", "half"), None, None),
            P(("groups", "sub", "half"), "scen", None),
            P(("groups", "sub", "half")),
            P(("groups", "sub", "half"), None, None),
            P(("groups", "sub", "half"), None, None),
            P(("groups", "sub", "half"), None, None),
            P(("groups", "sub", "half"), None, None),
            P(("groups", "sub", "half"), None, None),
            P(("groups", "scen")),
        ),
        out_specs=(P(("groups", "sub", "half"), "scen", None), P(None, ("groups", "scen"))),
        check_vma=False,
    )
```

```python
import jax
import jax.numpy as jnp
import numpy as np
from jax import lax
from jax.experimental import pallas as pl
from jax.experimental.pallas import tpu as pltpu
from jax.sharding import PartitionSpec as P

STEPS = 8
LANES = 128
VMEM_LIMIT = 16 * 2**20
HINT_FLOPS = 4 * 2**30
HINT_BYTES = 8 * 2**20
OWNER_AXES = ("sub", "half")
VARIANTS = (
    (2, 3, 0, 2),
    (2, 2, 3, 3),
    (4, 5, 0, 4),
    (2, 2, 0, 2),
    (0, 3, 0, 0),
    (4, 5, 3, 4),
)
NT = (((1,), (1,)), ((), ()))


def dot(left, right, dims=(((1,), (0,)), ((), ()))):
    return lax.dot_general(left, right, dims, preferred_element_type=jnp.float32)


def spread_matrix(column_count, owners):
    half = LANES // 2
    spread = np.zeros((LANES, (len(VARIANTS) + 2) * LANES), np.float32)
    for variant, gaps in enumerate(VARIANTS):
        for quarter, gap in enumerate(gaps):
            lane = variant * LANES + quarter * column_count
            for piece in range(3 * (gap - 2), 3 * (gap - 1)) if gap else ():
                for owner in range(owners):
                    spread[piece // 8 * half + owner * 8 + piece % 8, lane : lane + column_count] = 1
    for lane in range(LANES):
        for part in range(2):
            start = half + part * column_count
            spread[start + lane % column_count, (len(VARIANTS) + part) * LANES + lane] = 1
    return spread


SOURCES = (
    ((1, 2, 3, 0), (2, 3, 0, 1), (3, 0, 1, 2)),
    ((1, 3, 0, 2), (3, 2, 1, 0), (2, 0, 3, 1)),
)
HELD = (0, 3, 5, 7, 1, 2, 4, 6)


def spot_of(place, apart):
    if apart == 0:
        return 0
    spots = [1 + [p[z] for p in SOURCES[core]].index(z ^ apart) for z in range(4) for core in range(2)]
    bits = sum(spot << (2 * device) for device, spot in enumerate(spots))
    return (jnp.int32(bits) >> (2 * place)) & 3


def column_of(ref, place):
    _, peers, depth = ref.shape
    eye = lax.broadcasted_iota(jnp.int32, (depth, depth), 0) == lax.broadcasted_iota(
        jnp.int32, (depth, depth), 1
    )
    rows = [
        jnp.where(eye, jnp.broadcast_to(row.astype(jnp.float32), (depth, depth)), 0.0)
        for row in (ref[0, pl.ds(lax.bitwise_xor(place, jnp.int32(apart)), 1), :] for apart in range(peers))
    ]
    return jnp.sum(jnp.concatenate(rows, axis=0), axis=1, keepdims=True)


def owner_here():
    return lax.axis_index(OWNER_AXES[0]) * lax.axis_size(OWNER_AXES[1]) + lax.axis_index(OWNER_AXES[1])


def lane_kernel(lane_ref):
    lane_ref[...] = lax.broadcasted_iota(jnp.int32, lane_ref.shape, 1).astype(jnp.float32)


def pick_kernel(
    packed_ref, lane_ref, into_ref, from_ref, offset_ref, weight_ref, admit_ref, inverse_ref, cotangent_ref,
    message_ref, rows_ref,
):
    nodes = inverse_ref.shape[1]
    _, peers, depth = into_ref.shape
    slots = peers * depth
    columns = cotangent_ref.shape[1]
    lane_f = jnp.broadcast_to(lane_ref[:1], (slots, nodes))
    live = packed_ref[:, :1]
    alive = lane_f < live.astype(jnp.float32)
    place = owner_here()
    into = column_of(into_ref, place)
    source = column_of(from_ref, place)
    recv_hot = jnp.where((source == lane_f) & alive, 1.0, 0.0).astype(jnp.bfloat16)
    send_hot = jnp.where(into == lane_f, 1.0, 0.0).astype(jnp.bfloat16)
    driving = jnp.where(alive[:columns], cotangent_ref[0].astype(jnp.float32), 0.0).astype(jnp.bfloat16)
    stack = jnp.concatenate([recv_hot, driving], axis=0)
    picked = dot(stack, inverse_ref[0])
    lane = lax.broadcasted_iota(jnp.int32, picked.shape, 1)
    picked = jnp.where(lane < live, picked, 0.0).astype(jnp.bfloat16)
    width = columns + 1
    bus = (packed_ref[...] - place * nodes).astype(jnp.float32)
    eye = lax.broadcasted_iota(jnp.int32, (columns, width), 0) + 1 == lax.broadcasted_iota(
        jnp.int32, (columns, width), 1
    )
    bus = jnp.sum(jnp.where(eye, jnp.broadcast_to(bus, (columns, width)), 0.0), axis=1, keepdims=True)
    fault_hot = jnp.where(bus == lane_f[:columns], 1.0, 0.0).astype(jnp.bfloat16)
    delay = column_of(offset_ref, place)
    weight = column_of(weight_ref, place)
    admit = column_of(admit_ref, place)
    conduct = jnp.where(source >= 0, admit, 0.0)
    near, far = conduct * weight, conduct * (1.0 - weight)
    factors = [
        jnp.where(delay == 2, near, 0.0),
        jnp.where(delay == 3, near, 0.0) + jnp.where(delay == 2, far, 0.0),
        jnp.where(delay == 4, near, 0.0) + jnp.where(delay == 3, far, 0.0),
        jnp.where(delay == 4, far, 0.0),
    ]
    pieces = []
    for factor in factors:
        for _ in range(3):
            part = factor.astype(jnp.bfloat16).astype(jnp.float32)
            factor = factor - part
            pieces.append(part)
    spot = lax.broadcasted_iota(jnp.int32, (slots, LANES), 1)
    upper = jnp.zeros((slots, LANES), jnp.float32)
    lower = jnp.zeros((slots, LANES), jnp.float32)
    for index, piece in enumerate(pieces):
        if index < 8:
            upper = jnp.where(spot == index, piece, upper)
        else:
            lower = jnp.where(spot == index - 8, piece, lower)
    eye = jnp.where(
        lax.broadcasted_iota(jnp.int32, (8, LANES), 0) == lax.broadcasted_iota(jnp.int32, (8, LANES), 1), 1.0, 0.0
    ).astype(jnp.bfloat16)
    table = dot(eye, jnp.concatenate([upper, lower], axis=0).astype(jnp.bfloat16), NT)
    rows = picked[:slots]
    rows_ref[...] = rows
    blank = jnp.zeros((columns, nodes), jnp.bfloat16)
    body = dot(send_hot, jnp.concatenate([picked, blank], axis=0), NT) + dot(
        rows, jnp.concatenate([blank] * (slots // columns + 1) + [fault_hot], axis=0), NT
    )
    found = jnp.concatenate([blank] * (slots // columns) + [picked[slots:] * fault_hot, blank], axis=0)
    last = jnp.where(lax.broadcasted_iota(jnp.int32, (8, nodes), 0) == 7, 1.0, 0.0).astype(jnp.bfloat16)
    table = table + dot(last, found, NT)
    message_ref[...] = jnp.concatenate([body, table], axis=0).astype(jnp.bfloat16)


def lanes(value, index):
    return value[:, LANES * index : LANES * (index + 1)]


def turned_pieces(messages):
    slots = LANES // 2
    tables = [message[slots:].astype(jnp.float32) for message in messages]
    filled = tables + [jnp.zeros((8, LANES), jnp.float32)] * (8 - len(tables))
    turned = jnp.concatenate(filled * 2, axis=0).T
    lane = lax.broadcasted_iota(jnp.int32, (slots, LANES), 1)
    turned = jnp.where(lane < LANES // 2, turned[:slots], turned[slots:])
    group = lane % (LANES // 2) // 8
    return [jnp.where(group == index, turned, 0.0).astype(jnp.bfloat16) for index in range(len(messages))]


def widen_kernel(near_ref, spread_ref, wide_ref):
    place = owner_here()
    messages = [near_ref[spot_of(place, p)] for p in range(near_ref.shape[0])]
    count = LANES * len(VARIANTS)
    for index, piece in enumerate(turned_pieces(messages)):
        wide_ref[index, :, :count] = dot(piece, spread_ref[:, :count])
        wide_ref[index, :, count:] = dot(messages[index][: LANES // 2], spread_ref[:, count:])


def march_kernel(
    near_ref, far_ref, wide_ref, spread_ref, rows_ref, first_hbm, fault_hbm, first_ref, fault_ref, semaphores
):
    place = owner_here()
    held = ((near_ref, place), (far_ref, lax.bitwise_xor(place, jnp.int32(1))))
    owners = sum(ref.shape[0] for ref, _ in held)
    slots = rows_ref.shape[0]
    columns = first_ref.shape[1]
    depth = slots // owners
    count = len(VARIANTS)
    order = HELD
    spot = {apart: index for index, apart in enumerate(order)}

    def exchange(parts):
        return [
            jnp.concatenate(
                [parts[spot[mine ^ other]][depth * other : depth * (other + 1)] for other in range(owners)], axis=0
            )
            for mine in order
        ]

    def rounded(value):
        return value.astype(jnp.bfloat16).astype(jnp.float32)

    blocks = [ref[spot_of(holder, p)] for ref, holder in held for p in range(ref.shape[0])]
    system = [block[:slots, :slots] for block in blocks]
    fresh = blocks[-far_ref.shape[0] :]
    pieces = turned_pieces(fresh)

    def spread_of(index, sources):
        pair = slice(LANES * index, LANES * (index + 2))
        known = [wide_ref[p, :, pair] for p in range(wide_ref.shape[0])]
        both = known + [dot(source, spread_ref[:, pair]) for source in sources]
        return [lanes(part, 0) for part in both], [lanes(part, 1) for part in both]

    seven, fault = spread_of(count, [block[:slots] for block in fresh])
    factor = [*spread_of(0, pieces)]
    seven = exchange(seven)

    def seen(drive):
        total = fault[0] * drive[0].astype(jnp.float32)
        for o in range(1, owners):
            total = total + fault[o] * drive[o].astype(jnp.float32)
        return rounded(jnp.sum(total, axis=0, keepdims=True))

    near = [(factor[0][o] * seven[o]).astype(jnp.bfloat16) for o in range(owners)]
    wide = [(factor[1][o] * seven[o]).astype(jnp.bfloat16) for o in range(owners)]
    result = [dot(system[o], jnp.concatenate([near[o], wide[o]], axis=1)) for o in range(owners)]
    factor += [*spread_of(2, pieces), *spread_of(4, pieces)]
    row_a = seen(near)
    arrived = exchange([rounded(part) for part in result])
    drive = [
        factor[2][o] * seven[o] + factor[3][o] * lanes(arrived[o], 0) + factor[4][o] * lanes(arrived[o], 1)
        for o in range(owners)
    ]
    drive = [part.astype(jnp.bfloat16) for part in drive]
    later = [factor[5][o] * lanes(arrived[o], 1) for o in range(owners)]
    result = [dot(system[o], drive[o]) for o in range(owners)]
    row_b = seen(drive)
    arrived = exchange([rounded(part) for part in result])
    later = [later[o] + factor[1][o] * arrived[o] for o in range(owners)]
    turned = later[0].T
    own = (turned[columns : 2 * columns] + turned[3 * columns :]).astype(jnp.bfloat16)
    first_ref[0] = dot(own, rows_ref[...]).astype(jnp.bfloat16)
    save_first = pltpu.make_async_copy(first_ref, first_hbm, semaphores.at[0])
    save_first.start()
    row_c = seen([(part + pltpu.roll(part, 2 * columns, 1)).astype(jnp.bfloat16) for part in later])
    row_s = sum(block[slots + 7 : slots + 8].astype(jnp.float32) for block in blocks)

    def back(value, quarters):
        return pltpu.roll(value, LANES - quarters * columns, 1)

    table = [
        back(row_c, 1),
        row_c,
        back(row_b, 1),
        row_b,
        back(row_a, 1),
        row_a,
        jnp.zeros_like(row_a),
        back(row_s, 2),
    ]
    step = lax.broadcasted_iota(jnp.int32, (STEPS, LANES), 0)
    total = jnp.zeros((STEPS, LANES), jnp.float32)
    for index, value in enumerate(table):
        total = jnp.where(step == index, jnp.broadcast_to(value, total.shape), total)
    fault_ref[...] = total[:, :columns]
    save_fault = pltpu.make_async_copy(fault_ref, fault_hbm, semaphores.at[1])
    save_fault.start()
    save_first.wait()
    save_fault.wait()


def gathered_plan(
    inverses, cotangent, subnet_sizes, slot_into, slot_from, offsets, weights, admittance, fault_bus
):
    _, columns, nodes = cotangent.shape
    owners, depth = slot_into.shape[1:]
    slots = owners * depth
    height = slots + 8
    vmem = pl.BlockSpec(memory_space=pltpu.VMEM)
    hbm = pl.BlockSpec(memory_space=pltpu.HBM)
    lane = pl.pallas_call(
        lane_kernel,
        out_shape=jax.ShapeDtypeStruct((8, nodes), jnp.float32),
        out_specs=vmem,
        compiler_params=pltpu.CompilerParams(vmem_limit_bytes=VMEM_LIMIT),
        cost_estimate=pl.CostEstimate(flops=HINT_FLOPS, bytes_accessed=HINT_BYTES, transcendentals=0),
        name="lane",
    )()
    packed = jnp.concatenate([subnet_sizes, fault_bus])[None]
    arrays = (packed, lane, slot_into, slot_from, offsets, weights, admittance, inverses, cotangent)
    message, rows = pl.pallas_call(
        pick_kernel,
        out_shape=(
            jax.ShapeDtypeStruct((height, LANES), jnp.bfloat16),
            jax.ShapeDtypeStruct((slots, nodes), jnp.bfloat16),
        ),
        in_specs=[vmem] * len(arrays),
        out_specs=(vmem, vmem),
        compiler_params=pltpu.CompilerParams(vmem_limit_bytes=VMEM_LIMIT),
        name="pick",
    )(*arrays)
    spread = jnp.asarray(spread_matrix(columns, 8), jnp.bfloat16)
    width = spread.shape[1]


    def send(held, *sources):
        pairs = [(2 * sources[core][z] + 1 - core, 2 * z + core) for z in range(4) for core in range(2)]
        return lax.ppermute(held, OWNER_AXES, pairs)

    own = message[None]
    near = jnp.concatenate([own] + [send(own, *pair) for pair in zip(*SOURCES)], axis=0)
    far = send(near, range(4), range(4))
    wide = pl.pallas_call(
        widen_kernel,
        out_shape=jax.ShapeDtypeStruct((near.shape[0], slots, width), jnp.float32),
        in_specs=[vmem] * 2,
        out_specs=vmem,
        compiler_params=pltpu.CompilerParams(vmem_limit_bytes=VMEM_LIMIT),
        cost_estimate=pl.CostEstimate(
            flops=2 * near.shape[0] * slots * LANES * width, bytes_accessed=4 * near.shape[0] * slots * width, transcendentals=0
        ),
        name="widen",
    )(near, spread)
    outputs = (
        jax.ShapeDtypeStruct((1, columns, nodes), jnp.bfloat16),
        jax.ShapeDtypeStruct((STEPS, columns), jnp.float32),
    )
    return pl.pallas_call(
        march_kernel,
        out_shape=outputs,
        in_specs=[vmem] * 5,
        out_specs=(hbm, hbm),
        scratch_shapes=[
            *(pltpu.VMEM(output.shape, output.dtype) for output in outputs),
            pltpu.SemaphoreType.DMA((2,)),
        ],
        compiler_params=pltpu.CompilerParams(vmem_limit_bytes=VMEM_LIMIT),
        name="march",
    )(near, far, wide, spread, rows)


def exchanged_plan(
    inverses, cotangent, subnet_sizes, slot_into, slot_from, offsets, weights, admittance, fault_bus
):
    block_count, column_count, node_count = cotangent.shape
    owner_count = lax.axis_size(OWNER_AXES)
    slot_depth = slot_into.shape[2]
    slot_count = owner_count * slot_depth
    local_span = block_count * node_count
    active = (jnp.arange(node_count, dtype=jnp.int32)[None, :] < subnet_sizes[:, None]).astype(
        jnp.float32
    )
    node_ids = jnp.arange(local_span, dtype=jnp.int32)[None, :]
    send_hot = (slot_into.reshape(slot_count)[:, None] == node_ids).astype(jnp.bfloat16)
    send_hot = send_hot.reshape(slot_count, block_count, node_count)
    from_local = slot_from.reshape(slot_count)
    is_used = (from_local >= 0).astype(jnp.float32)
    recv_hot = (
        (from_local[:, None] == node_ids)
        .astype(jnp.float32)
        .reshape(slot_count, block_count, node_count)
    )
    delay_steps = offsets.reshape(slot_count)
    fraction = weights.reshape(slot_count)
    conduct = admittance.reshape(slot_count) * is_used
    arrivals = {}
    results = {}
    for step_now in range(STEPS - 1, -1, -1):
        history = jnp.zeros((block_count, column_count, node_count), jnp.float32)
        terms = jnp.zeros((column_count, slot_count), jnp.float32)
        present = False
        for source_step in range(step_now + 2, min(step_now + 6, STEPS)):
            step_gap = source_step - step_now
            factor = conduct * (
                fraction * (delay_steps == step_gap).astype(jnp.float32)
                + (1.0 - fraction) * (delay_steps + 1 == step_gap).astype(jnp.float32)
            )
            terms = terms + factor[None, :] * arrivals[source_step].astype(jnp.float32)
            present = True
        if present:
            history = jnp.einsum("sk,kjn->jsn", terms, recv_hot, precision=lax.Precision.HIGHEST)
        if step_now == STEPS - 1:
            history = cotangent.astype(jnp.float32)
        driving = (history * active[:, None, :]).astype(jnp.bfloat16)
        adjoint = jnp.einsum("jsn,jnm->jsm", driving, inverses, preferred_element_type=jnp.float32)
        results[step_now] = (adjoint * active[:, None, :]).astype(jnp.bfloat16)
        if step_now >= 2:
            picked = jnp.einsum(
                "jsn,kjn->sk", results[step_now], send_hot, preferred_element_type=jnp.float32
            )
            arrivals[step_now] = lax.all_to_all(
                picked.astype(jnp.bfloat16)[None], OWNER_AXES, split_axis=2, concat_axis=2, tiled=True
            )[0]
    owner_index = lax.axis_index(OWNER_AXES)
    local_bus = fault_bus - owner_index * local_span
    owned = (local_bus >= 0) & (local_bus < local_span)
    clamped = jnp.clip(local_bus, 0, local_span - 1)
    position = (
        clamped // node_count * column_count * node_count
        + jnp.arange(column_count, dtype=jnp.int32) * node_count
        + clamped % node_count
    )
    sensitivity = jnp.stack(
        [
            jnp.where(
                owned, jnp.take(results[index].reshape(-1), position).astype(jnp.float32), 0.0
            )
            for index in range(STEPS)
        ]
    )
    return results[0], lax.psum(sensitivity, OWNER_AXES)


def per_device(*arrays):
    blocks, columns, nodes = arrays[1].shape
    owners, depth = arrays[3].shape[1:]
    slots = owners * depth
    fits = (
        blocks == 1
        and columns * 4 == LANES
        and depth == 8
        and lax.axis_size(OWNER_AXES[0]) == 4
        and lax.axis_size(OWNER_AXES[1]) == 2
        and slots + 2 * columns == LANES
        and nodes % LANES == 0
    )
    return gathered_plan(*arrays) if fits else exchanged_plan(*arrays)


def solution(mesh):
    return jax.shard_map(
        per_device,
        mesh=mesh,
        in_specs=(
            P(("groups", "sub", "half"), None, None),
            P(("groups", "sub", "half"), "scen", None),
            P(("groups", "sub", "half")),
            P(("groups", "sub", "half"), None, None),
            P(("groups", "sub", "half"), None, None),
            P(("groups", "sub", "half"), None, None),
            P(("groups", "sub", "half"), None, None),
            P(("groups", "sub", "half"), None, None),
            P(("groups", "scen")),
        ),
        out_specs=(P(("groups", "sub", "half"), "scen", None), P(None, ("groups", "scen"))),
        check_vma=False,
    )
```

```python
import jax
import jax.numpy as jnp
import numpy as np
from jax import lax
from jax.experimental import pallas as pl
from jax.experimental.pallas import tpu as pltpu
from jax.sharding import PartitionSpec as P

STEPS = 8
LANES = 128
VMEM_LIMIT = 16 * 2**20
HINT_FLOPS = 4 * 2**30
HINT_BYTES = 8 * 2**20
OWNER_AXES = ("sub", "half")
VARIANTS = (
    (2, 3, 0, 2),
    (2, 2, 3, 3),
    (4, 5, 0, 4),
    (2, 2, 0, 2),
    (0, 3, 0, 0),
    (4, 5, 3, 4),
)
NT = (((1,), (1,)), ((), ()))


def dot(left, right, dims=(((1,), (0,)), ((), ()))):
    return lax.dot_general(left, right, dims, preferred_element_type=jnp.float32)


def spread_matrix(column_count, owners):
    half = LANES // 2
    spread = np.zeros((LANES, (len(VARIANTS) + 2) * LANES), np.float32)
    for variant, gaps in enumerate(VARIANTS):
        for quarter, gap in enumerate(gaps):
            lane = variant * LANES + quarter * column_count
            for piece in range(3 * (gap - 2), 3 * (gap - 1)) if gap else ():
                for owner in range(owners):
                    spread[piece // 8 * half + owner * 8 + piece % 8, lane : lane + column_count] = 1
    for lane in range(LANES):
        for part in range(2):
            start = half + part * column_count
            spread[start + lane % column_count, (len(VARIANTS) + part) * LANES + lane] = 1
    return spread


SOURCES = (
    ((1, 2, 3, 0), (2, 3, 0, 1), (3, 0, 1, 2)),
    ((1, 3, 0, 2), (3, 2, 1, 0), (2, 0, 3, 1)),
)
HELD = (0, 3, 5, 7, 1, 2, 4, 6)


def spot_of(place, apart):
    if apart == 0:
        return 0
    spots = [1 + [p[z] for p in SOURCES[core]].index(z ^ apart) for z in range(4) for core in range(2)]
    bits = sum(spot << (2 * device) for device, spot in enumerate(spots))
    return (jnp.int32(bits) >> (2 * place)) & 3


def column_of(ref, place):
    _, peers, depth = ref.shape
    eye = lax.broadcasted_iota(jnp.int32, (depth, depth), 0) == lax.broadcasted_iota(
        jnp.int32, (depth, depth), 1
    )
    rows = [
        jnp.where(eye, jnp.broadcast_to(row.astype(jnp.float32), (depth, depth)), 0.0)
        for row in (ref[0, pl.ds(lax.bitwise_xor(place, jnp.int32(apart)), 1), :] for apart in range(peers))
    ]
    return jnp.sum(jnp.concatenate(rows, axis=0), axis=1, keepdims=True)


def owner_here():
    return lax.axis_index(OWNER_AXES[0]) * lax.axis_size(OWNER_AXES[1]) + lax.axis_index(OWNER_AXES[1])


def lane_kernel(lane_ref):
    lane_ref[...] = lax.broadcasted_iota(jnp.int32, lane_ref.shape, 1).astype(jnp.float32)


def pick_kernel(
    packed_ref, lane_ref, into_ref, from_ref, offset_ref, weight_ref, admit_ref, inverse_ref, cotangent_ref,
    message_ref, rows_ref,
):
    nodes = inverse_ref.shape[1]
    _, peers, depth = into_ref.shape
    slots = peers * depth
    columns = cotangent_ref.shape[1]
    lane_f = jnp.broadcast_to(lane_ref[:1], (slots, nodes))
    live = packed_ref[:, :1]
    alive = lane_f < live.astype(jnp.float32)
    place = owner_here()
    into = column_of(into_ref, place)
    source = column_of(from_ref, place)
    recv_hot = jnp.where((source == lane_f) & alive, 1.0, 0.0).astype(jnp.bfloat16)
    send_hot = jnp.where(into == lane_f, 1.0, 0.0).astype(jnp.bfloat16)
    driving = jnp.where(alive[:columns], cotangent_ref[0].astype(jnp.float32), 0.0).astype(jnp.bfloat16)
    stack = jnp.concatenate([recv_hot, driving], axis=0)
    picked = dot(stack, inverse_ref[0])
    lane = lax.broadcasted_iota(jnp.int32, picked.shape, 1)
    picked = jnp.where(lane < live, picked, 0.0).astype(jnp.bfloat16)
    width = columns + 1
    bus = (packed_ref[...] - place * nodes).astype(jnp.float32)
    eye = lax.broadcasted_iota(jnp.int32, (columns, width), 0) + 1 == lax.broadcasted_iota(
        jnp.int32, (columns, width), 1
    )
    bus = jnp.sum(jnp.where(eye, jnp.broadcast_to(bus, (columns, width)), 0.0), axis=1, keepdims=True)
    fault_hot = jnp.where(bus == lane_f[:columns], 1.0, 0.0).astype(jnp.bfloat16)
    delay = column_of(offset_ref, place)
    weight = column_of(weight_ref, place)
    admit = column_of(admit_ref, place)
    conduct = jnp.where(source >= 0, admit, 0.0)
    near, far = conduct * weight, conduct * (1.0 - weight)
    factors = [
        jnp.where(delay == 2, near, 0.0),
        jnp.where(delay == 3, near, 0.0) + jnp.where(delay == 2, far, 0.0),
        jnp.where(delay == 4, near, 0.0) + jnp.where(delay == 3, far, 0.0),
        jnp.where(delay == 4, far, 0.0),
    ]
    pieces = []
    for factor in factors:
        for _ in range(3):
            part = factor.astype(jnp.bfloat16).astype(jnp.float32)
            factor = factor - part
            pieces.append(part)
    spot = lax.broadcasted_iota(jnp.int32, (slots, LANES), 1)
    upper = jnp.zeros((slots, LANES), jnp.float32)
    lower = jnp.zeros((slots, LANES), jnp.float32)
    for index, piece in enumerate(pieces):
        if index < 8:
            upper = jnp.where(spot == index, piece, upper)
        else:
            lower = jnp.where(spot == index - 8, piece, lower)
    eye = jnp.where(
        lax.broadcasted_iota(jnp.int32, (8, LANES), 0) == lax.broadcasted_iota(jnp.int32, (8, LANES), 1), 1.0, 0.0
    ).astype(jnp.bfloat16)
    table = dot(eye, jnp.concatenate([upper, lower], axis=0).astype(jnp.bfloat16), NT)
    rows = picked[:slots]
    rows_ref[...] = rows
    blank = jnp.zeros((columns, nodes), jnp.bfloat16)
    body = dot(send_hot, jnp.concatenate([picked, blank], axis=0), NT) + dot(
        rows, jnp.concatenate([blank] * (slots // columns + 1) + [fault_hot], axis=0), NT
    )
    found = jnp.concatenate([blank] * (slots // columns) + [picked[slots:] * fault_hot, blank], axis=0)
    last = jnp.where(lax.broadcasted_iota(jnp.int32, (8, nodes), 0) == 7, 1.0, 0.0).astype(jnp.bfloat16)
    table = table + dot(last, found, NT)
    message_ref[...] = jnp.concatenate([body, table], axis=0).astype(jnp.bfloat16)


def lanes(value, index):
    return value[:, LANES * index : LANES * (index + 1)]


def turned_pieces(messages):
    slots = LANES // 2
    tables = [message[slots:].astype(jnp.float32) for message in messages]
    filled = tables + [jnp.zeros((8, LANES), jnp.float32)] * (8 - len(tables))
    turned = jnp.concatenate(filled * 2, axis=0).T
    lane = lax.broadcasted_iota(jnp.int32, (slots, LANES), 1)
    turned = jnp.where(lane < LANES // 2, turned[:slots], turned[slots:])
    group = lane % (LANES // 2) // 8
    return [jnp.where(group == index, turned, 0.0).astype(jnp.bfloat16) for index in range(len(messages))]


def widen_kernel(near_ref, spread_ref, wide_ref):
    place = owner_here()
    messages = [near_ref[spot_of(place, p)] for p in range(near_ref.shape[0])]
    count = LANES * len(VARIANTS)
    for index, piece in enumerate(turned_pieces(messages)):
        wide_ref[index, :, :count] = dot(piece, spread_ref[:, :count])
        wide_ref[index, :, count:] = dot(messages[index][: LANES // 2], spread_ref[:, count:])


def march_kernel(
    near_ref, far_ref, wide_ref, spread_ref, rows_ref, first_hbm, fault_hbm, first_ref, fault_ref, semaphores
):
    place = owner_here()
    held = ((near_ref, place), (far_ref, lax.bitwise_xor(place, jnp.int32(1))))
    owners = sum(ref.shape[0] for ref, _ in held)
    slots = rows_ref.shape[0]
    columns = first_ref.shape[1]
    depth = slots // owners
    count = len(VARIANTS)
    order = HELD
    spot = {apart: index for index, apart in enumerate(order)}

    def exchange(parts):
        return [
            jnp.concatenate(
                [parts[spot[mine ^ other]][depth * other : depth * (other + 1)] for other in range(owners)], axis=0
            )
            for mine in order
        ]

    def rounded(value):
        return value.astype(jnp.bfloat16).astype(jnp.float32)

    blocks = [ref[spot_of(holder, p)] for ref, holder in held for p in range(ref.shape[0])]
    system = [block[:slots, :slots] for block in blocks]
    fresh = blocks[-far_ref.shape[0] :]
    pieces = turned_pieces(fresh)

    def spread_of(index, sources):
        pair = slice(LANES * index, LANES * (index + 2))
        known = [wide_ref[p, :, pair] for p in range(wide_ref.shape[0])]
        both = known + [dot(source, spread_ref[:, pair]) for source in sources]
        return [lanes(part, 0) for part in both], [lanes(part, 1) for part in both]

    seven, fault = spread_of(count, [block[:slots] for block in fresh])
    factor = [*spread_of(0, pieces)]
    seven = exchange(seven)

    def seen(drive):
        total = fault[0] * drive[0].astype(jnp.float32)
        for o in range(1, owners):
            total = total + fault[o] * drive[o].astype(jnp.float32)
        return rounded(jnp.sum(total, axis=0, keepdims=True))

    near = [(factor[0][o] * seven[o]).astype(jnp.bfloat16) for o in range(owners)]
    wide = [(factor[1][o] * seven[o]).astype(jnp.bfloat16) for o in range(owners)]
    result = [dot(system[o], jnp.concatenate([near[o], wide[o]], axis=1)) for o in range(owners)]
    factor += [*spread_of(2, pieces)]
    arrived = exchange([rounded(part) for part in result])
    factor += [*spread_of(4, pieces)]
    row_a = seen(near)
    drive = [
        factor[2][o] * seven[o] + factor[3][o] * lanes(arrived[o], 0) + factor[4][o] * lanes(arrived[o], 1)
        for o in range(owners)
    ]
    drive = [part.astype(jnp.bfloat16) for part in drive]
    later = [factor[5][o] * lanes(arrived[o], 1) for o in range(owners)]
    result = [dot(system[o], drive[o]) for o in range(owners)]
    row_b = seen(drive)
    arrived = exchange([rounded(part) for part in result])
    later = [later[o] + factor[1][o] * arrived[o] for o in range(owners)]
    turned = later[0].T
    own = (turned[columns : 2 * columns] + turned[3 * columns :]).astype(jnp.bfloat16)
    first_ref[0] = dot(own, rows_ref[...]).astype(jnp.bfloat16)
    save_first = pltpu.make_async_copy(first_ref, first_hbm, semaphores.at[0])
    save_first.start()
    row_c = seen([(part + pltpu.roll(part, 2 * columns, 1)).astype(jnp.bfloat16) for part in later])
    row_s = sum(block[slots + 7 : slots + 8].astype(jnp.float32) for block in blocks)

    def back(value, quarters):
        return pltpu.roll(value, LANES - quarters * columns, 1)

    table = [
        back(row_c, 1),
        row_c,
        back(row_b, 1),
        row_b,
        back(row_a, 1),
        row_a,
        jnp.zeros_like(row_a),
        back(row_s, 2),
    ]
    step = lax.broadcasted_iota(jnp.int32, (STEPS, LANES), 0)
    total = jnp.zeros((STEPS, LANES), jnp.float32)
    for index, value in enumerate(table):
        total = jnp.where(step == index, jnp.broadcast_to(value, total.shape), total)
    fault_ref[...] = total[:, :columns]
    save_fault = pltpu.make_async_copy(fault_ref, fault_hbm, semaphores.at[1])
    save_fault.start()
    save_first.wait()
    save_fault.wait()


def gathered_plan(
    inverses, cotangent, subnet_sizes, slot_into, slot_from, offsets, weights, admittance, fault_bus
):
    _, columns, nodes = cotangent.shape
    owners, depth = slot_into.shape[1:]
    slots = owners * depth
    height = slots + 8
    vmem = pl.BlockSpec(memory_space=pltpu.VMEM)
    hbm = pl.BlockSpec(memory_space=pltpu.HBM)
    lane = pl.pallas_call(
        lane_kernel,
        out_shape=jax.ShapeDtypeStruct((8, nodes), jnp.float32),
        out_specs=vmem,
        compiler_params=pltpu.CompilerParams(vmem_limit_bytes=VMEM_LIMIT),
        cost_estimate=pl.CostEstimate(flops=HINT_FLOPS, bytes_accessed=HINT_BYTES, transcendentals=0),
        name="lane",
    )()
    packed = jnp.concatenate([subnet_sizes, fault_bus])[None]
    arrays = (packed, lane, slot_into, slot_from, offsets, weights, admittance, inverses, cotangent)
    message, rows = pl.pallas_call(
        pick_kernel,
        out_shape=(
            jax.ShapeDtypeStruct((height, LANES), jnp.bfloat16),
            jax.ShapeDtypeStruct((slots, nodes), jnp.bfloat16),
        ),
        in_specs=[vmem] * len(arrays),
        out_specs=(vmem, vmem),
        compiler_params=pltpu.CompilerParams(vmem_limit_bytes=VMEM_LIMIT),
        name="pick",
    )(*arrays)
    spread = jnp.asarray(spread_matrix(columns, 8), jnp.bfloat16)
    width = spread.shape[1]


    def send(held, *sources):
        pairs = [(2 * sources[core][z] + 1 - core, 2 * z + core) for z in range(4) for core in range(2)]
        return lax.ppermute(held, OWNER_AXES, pairs)

    own = message[None]
    near = jnp.concatenate([own] + [send(own, *pair) for pair in zip(*SOURCES)], axis=0)
    far = send(near, range(4), range(4))
    wide = pl.pallas_call(
        widen_kernel,
        out_shape=jax.ShapeDtypeStruct((near.shape[0], slots, width), jnp.float32),
        in_specs=[vmem] * 2,
        out_specs=vmem,
        compiler_params=pltpu.CompilerParams(vmem_limit_bytes=VMEM_LIMIT),
        cost_estimate=pl.CostEstimate(
            flops=2 * near.shape[0] * slots * LANES * width, bytes_accessed=4 * near.shape[0] * slots * width, transcendentals=0
        ),
        name="widen",
    )(near, spread)
    outputs = (
        jax.ShapeDtypeStruct((1, columns, nodes), jnp.bfloat16),
        jax.ShapeDtypeStruct((STEPS, columns), jnp.float32),
    )
    return pl.pallas_call(
        march_kernel,
        out_shape=outputs,
        in_specs=[vmem] * 5,
        out_specs=(hbm, hbm),
        scratch_shapes=[
            *(pltpu.VMEM(output.shape, output.dtype) for output in outputs),
            pltpu.SemaphoreType.DMA((2,)),
        ],
        compiler_params=pltpu.CompilerParams(vmem_limit_bytes=VMEM_LIMIT),
        name="march",
    )(near, far, wide, spread, rows)


def exchanged_plan(
    inverses, cotangent, subnet_sizes, slot_into, slot_from, offsets, weights, admittance, fault_bus
):
    block_count, column_count, node_count = cotangent.shape
    owner_count = lax.axis_size(OWNER_AXES)
    slot_depth = slot_into.shape[2]
    slot_count = owner_count * slot_depth
    local_span = block_count * node_count
    active = (jnp.arange(node_count, dtype=jnp.int32)[None, :] < subnet_sizes[:, None]).astype(
        jnp.float32
    )
    node_ids = jnp.arange(local_span, dtype=jnp.int32)[None, :]
    send_hot = (slot_into.reshape(slot_count)[:, None] == node_ids).astype(jnp.bfloat16)
    send_hot = send_hot.reshape(slot_count, block_count, node_count)
    from_local = slot_from.reshape(slot_count)
    is_used = (from_local >= 0).astype(jnp.float32)
    recv_hot = (
        (from_local[:, None] == node_ids)
        .astype(jnp.float32)
        .reshape(slot_count, block_count, node_count)
    )
    delay_steps = offsets.reshape(slot_count)
    fraction = weights.reshape(slot_count)
    conduct = admittance.reshape(slot_count) * is_used
    arrivals = {}
    results = {}
    for step_now in range(STEPS - 1, -1, -1):
        history = jnp.zeros((block_count, column_count, node_count), jnp.float32)
        terms = jnp.zeros((column_count, slot_count), jnp.float32)
        present = False
        for source_step in range(step_now + 2, min(step_now + 6, STEPS)):
            step_gap = source_step - step_now
            factor = conduct * (
                fraction * (delay_steps == step_gap).astype(jnp.float32)
                + (1.0 - fraction) * (delay_steps + 1 == step_gap).astype(jnp.float32)
            )
            terms = terms + factor[None, :] * arrivals[source_step].astype(jnp.float32)
            present = True
        if present:
            history = jnp.einsum("sk,kjn->jsn", terms, recv_hot, precision=lax.Precision.HIGHEST)
        if step_now == STEPS - 1:
            history = cotangent.astype(jnp.float32)
        driving = (history * active[:, None, :]).astype(jnp.bfloat16)
        adjoint = jnp.einsum("jsn,jnm->jsm", driving, inverses, preferred_element_type=jnp.float32)
        results[step_now] = (adjoint * active[:, None, :]).astype(jnp.bfloat16)
        if step_now >= 2:
            picked = jnp.einsum(
                "jsn,kjn->sk", results[step_now], send_hot, preferred_element_type=jnp.float32
            )
            arrivals[step_now] = lax.all_to_all(
                picked.astype(jnp.bfloat16)[None], OWNER_AXES, split_axis=2, concat_axis=2, tiled=True
            )[0]
    owner_index = lax.axis_index(OWNER_AXES)
    local_bus = fault_bus - owner_index * local_span
    owned = (local_bus >= 0) & (local_bus < local_span)
    clamped = jnp.clip(local_bus, 0, local_span - 1)
    position = (
        clamped // node_count * column_count * node_count
        + jnp.arange(column_count, dtype=jnp.int32) * node_count
        + clamped % node_count
    )
    sensitivity = jnp.stack(
        [
            jnp.where(
                owned, jnp.take(results[index].reshape(-1), position).astype(jnp.float32), 0.0
            )
            for index in range(STEPS)
        ]
    )
    return results[0], lax.psum(sensitivity, OWNER_AXES)


def per_device(*arrays):
    blocks, columns, nodes = arrays[1].shape
    owners, depth = arrays[3].shape[1:]
    slots = owners * depth
    fits = (
        blocks == 1
        and columns * 4 == LANES
        and depth == 8
        and lax.axis_size(OWNER_AXES[0]) == 4
        and lax.axis_size(OWNER_AXES[1]) == 2
        and slots + 2 * columns == LANES
        and nodes % LANES == 0
    )
    return gathered_plan(*arrays) if fits else exchanged_plan(*arrays)


def solution(mesh):
    return jax.shard_map(
        per_device,
        mesh=mesh,
        in_specs=(
            P(("groups", "sub", "half"), None, None),
            P(("groups", "sub", "half"), "scen", None),
            P(("groups", "sub", "half")),
            P(("groups", "sub", "half"), None, None),
            P(("groups", "sub", "half"), None, None),
            P(("groups", "sub", "half"), None, None),
            P(("groups", "sub", "half"), None, None),
            P(("groups", "sub", "half"), None, None),
            P(("groups", "scen")),
        ),
        out_specs=(P(("groups", "sub", "half"), "scen", None), P(None, ("groups", "scen"))),
        check_vma=False,
    )
```
